256 devices in a mesh: dp: 64 (over z, x, core), tensor: 4 (over y).
Axes of the slice: x: 4, y: 4, z: 8, core: 2. Of those that a mesh axis runs over, the one named last changes fastest.
Arguments:
- momentum: float32 [12288, 26624], P('dp', 'tensor'), may hold values from -45 to 45
- gradient: bfloat16 [12288, 26624], P('dp', 'tensor'), may hold values from -6 to 6
- right_prev: float32 [26624, 128], P(('tensor', 'dp')), may hold values from -0.0390625 to 0.0390625
Outputs:
- new_momentum: float32 [12288, 26624], P('dp', 'tensor')
- left_factor: float32 [12288, 128], P('dp')
- right_factor: float32 [26624, 128], P(('tensor', 'dp'))
The draws below stay inside these ranges and needn't reach their ends.
All inputs are finite; a program needn't handle non-finite values.
Results may differ from the reference program's by a relative error of at most 0.0003.
Values sent between devices are 32-bit elements; how exact they have to be, the bound alone decides.
A program may use at most 64 MiB of HBM per device.

```python
import jax
import jax.numpy as jnp
from jax import lax

NC = 26624
RANK = 128
MR = 12288


def draw_momentum(key, part):
    key = jax.random.fold_in(key, 11)
    first, second, third = jax.random.split(key, 3)
    row_scale = jnp.exp(jax.random.uniform(second, (MR, 1), jnp.float32, -1.15, 1.15))
    col_scale = jnp.exp(jax.random.uniform(third, (1, NC), jnp.float32, -1.15, 1.15))
    base = jnp.clip(jax.random.normal(first, (MR, NC), jnp.float32), -4.0, 4.0)
    return base * row_scale * col_scale


def shard_levels(rng, dims, cuts, low, top_value):
    factor_of, own = 1.0, jax.random.fold_in(rng, 6)
    for dim, shards_of in cuts:
        heights = jnp.exp(jax.random.uniform(jax.random.fold_in(own, dim), (shards_of,), jnp.float32, low / len(cuts), top_value / len(cuts)))
        factor_of = factor_of * jnp.repeat(heights, dims[dim] // shards_of).reshape([-1 if axis == dim else 1 for axis in range(len(dims))])
    return factor_of


def noise(key, dims, width, bound, cuts=(), held_as=jnp.bfloat16):
    loudness = shard_levels(key, dims, cuts, -0.22, 0.18) if cuts else 1.0
    values = jax.random.normal(key, dims, jnp.float32) * width * loudness
    return jnp.minimum(jnp.maximum(values, -bound), bound).astype(held_as)


def setup_inputs(seed: int = 0) -> dict:
    key_list = jax.random.split(jax.random.key(seed), 4)
    return {
        "momentum": draw_momentum(jax.random.fold_in(key_list[3], 71), 0),
        "gradient": noise(key_list[1], (MR, NC), 1.0, 6.0, ((0, 64), (1, 4))),
        "right_prev": noise(key_list[2], (NC, RANK), NC ** -0.5, 0.0390625, ((0, 256),), jnp.float32),
    }


HIGH = lax.Precision.HIGHEST

def upper_factor(gram):
    size = gram.shape[0]
    places = jnp.arange(size, dtype=jnp.int32)

    def advance(j, state):
        remain, upper = state
        row = lax.dynamic_slice_in_dim(remain, j, 1, 0)[0]
        pivot = jnp.sum(jnp.where(places == j, row, jnp.zeros_like(row)))
        urow = jnp.where(places >= j, row * lax.rsqrt(pivot), jnp.zeros_like(row))
        upper = lax.dynamic_update_slice_in_dim(upper, urow[None, :], j, 0)
        remain = remain - urow[:, None] * urow[None, :]
        return (remain, upper)
    start = (gram, jnp.zeros_like(gram))
    return lax.fori_loop(0, size, advance, start)[1]

def upper_inverse(upper):
    size = upper.shape[0]
    places = jnp.arange(size, dtype=jnp.int32)

    def advance(k, inverse):
        i = size - 1 - k
        row = lax.dynamic_slice_in_dim(upper, i, 1, 0)[0]
        diag_val = jnp.sum(jnp.where(places == i, row, jnp.zeros_like(row)))
        masked = jnp.where(places > i, row, jnp.zeros_like(row))
        unit = jnp.where(places == i, jnp.ones_like(row), jnp.zeros_like(row))
        inner = jnp.dot(masked[None, :], inverse, precision=HIGH, preferred_element_type=jnp.float32)[0]
        xrow = (unit - inner) / diag_val
        return lax.dynamic_update_slice_in_dim(inverse, xrow[None, :], i, 0)
    return lax.fori_loop(0, size, advance, jnp.zeros_like(upper))

def reference(momentum, gradient, right_prev):
    blend = momentum + gradient.astype(jnp.float32)
    projected = jnp.dot(blend, right_prev, precision=HIGH, preferred_element_type=jnp.float32)
    gram = jnp.dot(projected.T, projected, precision=HIGH, preferred_element_type=jnp.float32)
    upper = upper_factor(gram)
    inverse = upper_inverse(upper)
    left_factor = jnp.dot(projected, inverse, precision=HIGH, preferred_element_type=jnp.float32)
    coupled = jnp.dot(blend.T, left_factor, precision=HIGH, preferred_element_type=jnp.float32)
    squares = lax.optimization_barrier(jnp.sum(coupled * coupled, axis=0, keepdims=True))
    right_factor = coupled * lax.rsqrt(squares + 1e-06)
    new_momentum = blend - 0.05 * jnp.dot(left_factor, coupled.T, precision=HIGH, preferred_element_type=jnp.float32)
    return (new_momentum, left_factor, right_factor)
```

```python
import functools

import jax
import jax.numpy as jnp
from jax import lax
from jax.experimental import pallas as pl
from jax.experimental.pallas import tpu as pltpu
from jax.sharding import PartitionSpec as P

HIGHEST = lax.Precision.HIGHEST
MESH = pl.DeviceIdType.MESH
F32 = jnp.float32
BF16 = jnp.bfloat16
ROWS = 8
FIRST = 64
SIGNS = (1, -1)


def dot(a, b, dims, precision=None):
    return lax.dot_general(a, b, (dims, ((), ())), precision=precision, preferred_element_type=F32)


def split(value):
    high = value.astype(BF16)
    return high, (value - high.astype(F32)).astype(BF16)


def offsets(k, n):
    if k == 0 or 2 * k == n:
        return (k,)
    return (k, n - k)


class Place:
    def __init__(self, nz, nx, ny):
        self.nz, self.nx, self.ny = nz, nx, ny
        self.hz, self.hx = nz // 2, nx // 2
        at = lax.axis_index("dp")
        self.y = lax.axis_index("tensor")
        self.z, self.x, self.c = at // (2 * nx), (at // 2) % nx, at % 2

    def zr(self, o):
        return (self.z + (o + 2 * self.nz)) % self.nz

    def xr(self, o):
        return (self.x + (o + 2 * self.nx)) % self.nx

    def yr(self, o):
        return (self.y + (o + 2 * self.ny)) % self.ny

    def to(self, oz=0, ox=0, oy=0, oc=0):
        core = (self.c + oc) % 2
        return ((self.zr(oz) * self.nx + self.xr(ox)) * 2 + core, self.yr(oy))

    def partners(self):
        out = [dict(oc=1)]
        out += [dict(ox=o) for o in range(1, self.nx)]
        out += [dict(oz=o) for o in range(1, self.nz)]
        out += [dict(oy=o, oc=k) for o in range(1, self.ny) for k in range(2)]
        return out


class Wire:
    def __init__(self, send_sems, recv_sems):
        self.sems, self.names, self.sent = (send_sems, recv_sems), {}, []

    def copy(self, name, src, dst, device):
        at = self.names.setdefault(name, len(self.names))
        return pltpu.make_async_remote_copy(
            src_ref=src,
            dst_ref=dst,
            send_sem=self.sems[0].at[at],
            recv_sem=self.sems[1].at[at],
            device_id=device,
            device_id_type=MESH,
        )

    def send(self, name, src, dst, device):
        copy = self.copy(name, src, dst, device)
        copy.start()
        self.sent.append(copy)

    def got(self, name, dst, device):
        self.copy(name, dst, dst, device).wait_recv()

    def drain(self):
        for copy in self.sent:
            copy.wait_send()
        self.sent = []


def first_rows(d, half):
    if not half:
        return pl.ds(0, FIRST)
    return pl.ds(0 if d > 0 else FIRST // 2, FIRST // 2)


def rest_rows(d, half, start, depth):
    count = depth - FIRST
    if not half:
        return pl.ds(start, count)
    cut = (count // 16 + 1) * 8
    return pl.ds(start, cut) if d > 0 else pl.ds(start + cut, count - cut)


def some_x(d, half, nx):
    if not half:
        return pl.ds(0, nx)
    return pl.ds(0 if d > 0 else nx // 2, nx // 2)


def gather(at, wire, buf, between):
    hz, hx, nz, nx = at.hz, at.hx, at.nz, at.nx
    z, x, c, zr, xr = at.z, at.x, at.c, at.zr, at.xr
    depth = buf.shape[3]
    rest = pl.ds(FIRST, depth - FIRST)
    own = at.to()

    def send(name, ref, **where):
        wire.send(name, ref, ref, at.to(**where))

    def got(name, ref):
        wire.got(name, ref, own)

    for s in range(hz + hx + 1):
        for d in SIGNS:
            if 1 <= s <= hz:
                got(("bz", d, s), buf.at[zr(-d * s), x, c, first_rows(d, s == hz)])
            if s + 1 <= hz:
                send(("bz", d, s + 1), buf.at[zr(-d * s), x, c, first_rows(d, s + 1 == hz)], oz=d)
        for d in SIGNS:
            if 1 <= s <= hx:
                got(("ax", d, s), buf.at[z, xr(-d * s), c, rest_rows(d, s == hx, FIRST, depth)])
            if s + 1 <= hx:
                send(("ax", d, s + 1), buf.at[z, xr(-d * s), c, rest_rows(d, s + 1 == hx, FIRST, depth)], ox=d)
        for k in range(hz + 1):
            for o in offsets(k, nz):
                for d in SIGNS:
                    t = s - k
                    if 1 <= t <= hx:
                        got(("bx", o, d, t), buf.at[zr(o), xr(-d * t), c, first_rows(d, t == hx)])
                    if 1 <= t + 1 <= hx:
                        send(("bx", o, d, t + 1), buf.at[zr(o), xr(-d * t), c, first_rows(d, t + 1 == hx)], ox=d)
        for d in SIGNS:
            q = s - hx
            if 1 <= q <= hz:
                got(("az", d, q), buf.at[zr(-d * q), some_x(d, q == hz, nx), c, rest])
            if 1 <= q + 1 <= hz:
                send(("az", d, q + 1), buf.at[zr(-d * q), some_x(d, q + 1 == hz, nx), c, rest], oz=d)
        if s >= hx:
            for o in offsets(s - hx, nz):
                send(("both", o), buf.at[zr(o), :, c], oc=1)
        if s >= hx + 1:
            for o in offsets(s - hx - 1, nz):
                got(("both", o), buf.at[zr(o), :, 1 - c])
        between(s)
    for o in offsets(hz, nz):
        got(("both", o), buf.at[zr(o), :, 1 - c])


def reduce(at, wire, parts, sib, xb, zsum, zb, za, xsum, xa, make, between):
    hz, hx, nz, nx = at.hz, at.hx, at.nz, at.nx
    x, c, xr = at.x, at.c, at.xr
    depth = parts.shape[3]
    rest = pl.ds(FIRST, depth - FIRST)
    own = at.to()

    def terms(k):
        for o in offsets(k, nz):
            make(o)
            wire.send(("both", o), parts.at[o, :, 1 - c], sib.at[o], at.to(oc=1))

    terms(hz)
    for s in range(hz + hx + 1):
        if s < hz:
            terms(hz - s - 1)
        if s <= hz:
            for o in offsets(hz - s, nz):
                wire.got(("both", o), sib.at[o], own)
                parts[o, :, c] = parts[o, :, c] + sib[o]
        for k in range(hz, -1, -1):
            t = s - (hz - k) + 1
            for o in offsets(k, nz):
                for i, d in enumerate(SIGNS):
                    if 2 <= t <= hx + 1:
                        rows = first_rows(d, t == 2)
                        wire.got(("bx", o, d, t - 1), xb.at[o, i, t - 2, rows], own)
                        to = xr(d * (hx - t + 1))
                        parts[o, to, c, rows] = parts[o, to, c, rows] + xb[o, i, t - 2, rows]
                    if 1 <= t <= hx:
                        rows = first_rows(d, t == 1)
                        wire.send(
                            ("bx", o, d, t),
                            parts.at[o, xr(d * (hx - t + 1)), c, rows],
                            xb.at[o, i, t - 1, rows],
                            at.to(ox=d),
                        )
                if t == hx + 1:
                    zsum[o] = parts[o, x, c, pl.ds(0, FIRST)]
        q = s - hx + 1
        for i, d in enumerate(SIGNS):
            o = (d * (hz - q + 1)) % nz
            if 2 <= q <= hz + 1:
                rows = first_rows(d, q == 2)
                wire.got(("bz", d, q - 1), zb.at[i, q - 2, rows], own)
                zsum[o, rows] = zsum[o, rows] + zb[i, q - 2, rows]
            if 1 <= q <= hz:
                rows = first_rows(d, q == 1)
                wire.send(("bz", d, q), zsum.at[o, rows], zb.at[i, q - 1, rows], at.to(oz=d))
        q = s + 1
        for i, d in enumerate(SIGNS):
            o = (d * (hz - q + 1)) % nz
            if 2 <= q <= hz + 1:
                xs = some_x(d, q == 2, nx)
                wire.got(("az", d, q - 1), za.at[i, q - 2, xs], own)
                parts[o, xs, c, rest] = parts[o, xs, c, rest] + za[i, q - 2, xs]
            if 1 <= q <= hz:
                xs = some_x(d, q == 1, nx)
                wire.send(("az", d, q), parts.at[o, xs, c, rest], za.at[i, q - 1, xs], at.to(oz=d))
        if s == hz:
            xsum[...] = parts[0, :, c, rest]
        t = s - hz + 1
        for i, d in enumerate(SIGNS):
            if 2 <= t <= hx + 1:
                rows = rest_rows(d, t == 2, 0, depth)
                wire.got(("ax", d, t - 1), xa.at[i, t - 2, rows], own)
                to = xr(d * (hx - t + 1))
                xsum[to, rows] = xsum[to, rows] + xa[i, t - 2, rows]
            if 1 <= t <= hx:
                rows = rest_rows(d, t == 1, 0, depth)
                wire.send(
                    ("ax", d, t), xsum.at[xr(d * (hx - t + 1)), rows], xa.at[i, t - 1, rows], at.to(ox=d)
                )
        between(s)
    return zsum[0], xsum[x]


def invert_block(b, work, out_ref):
    size = out_ref.shape[0]
    start = pl.multiple_of(b * ROWS, ROWS)
    panel = work[pl.ds(start, ROWS), :]
    first = pltpu.roll(panel[:, :size], (size - start) % size, 1)
    g = {}
    for i in range(ROWS):
        for j in range(i, ROWS):
            g[i, j] = jnp.broadcast_to(first[i : i + 1, j : j + 1], (1, size))
    scale = []
    for k in range(ROWS):
        r = lax.rsqrt(g[k, k])
        scale.append(r)
        for j in range(k + 1, ROWS):
            g[k, j] = g[k, j] * r
        for i in range(k + 1, ROWS):
            for j in range(i, ROWS):
                g[i, j] = g[i, j] - g[k, i] * g[k, j]
    done = []
    for i in range(ROWS):
        left, right = panel[i : i + 1, :size], panel[i : i + 1, size:]
        for k in range(i):
            left = left - g[k, i] * done[k][0]
            right = right - g[k, i] * done[k][1]
        done.append((left * scale[i], right * scale[i]))
    upper = jnp.concatenate([d[0] for d in done], axis=0)
    inverse = jnp.concatenate([d[1] for d in done], axis=0)
    out_ref[pl.ds(start, ROWS), :] = inverse
    both = jnp.concatenate([upper, inverse], axis=1)
    work[...] = work[...] - dot(upper, both, ((0,), (0,)), HIGHEST)


def factors(
    nz, nx, ny, cuts,
    momentum, gradient, right_prev,
    left_ref, right_ref, coupled_ref,
    mom, grad, high, low, high_t, low_t, right, parts, sib, xb, zsum, zb, za, xsum, xa, whole,
    part, proj, yrecv, gram, work, inv, graw, gx, gz, gall, sq,
    load_sem, s1, r1, s2, r2, s3, r3, s4, r4,
):
    at = Place(nz, nx, ny)
    z, x, c, y = at.z, at.x, at.c, at.y
    own = at.to()
    rows, columns = mom.shape
    rank = proj.shape[1]
    wide = columns // cuts
    depth = right_prev.shape[0]
    share = rows // ny
    one, two, three, misc = Wire(s1, r1), Wire(s2, r2), Wire(s3, r3), Wire(s4, r4)

    loads = []
    for i in range(cuts):
        cut = pl.ds(i * wide, wide)
        for j, (src, dst) in enumerate(((momentum, mom), (gradient, grad))):
            copy = pltpu.make_async_copy(src.at[:, cut], dst.at[:, cut], load_sem.at[j, i])
            copy.start()
            loads.append(copy)

    partners = at.partners()
    barrier = pltpu.get_barrier_semaphore()
    for where in partners:
        pl.semaphore_signal(barrier, inc=1, device_id=at.to(**where), device_id_type=MESH)
    right[z, x, c] = right_prev[...]
    pl.semaphore_wait(barrier, len(partners))

    def prepare(s):
        if not 0 <= s < cuts:
            return
        loads[2 * s].wait()
        loads[2 * s + 1].wait()
        tile = 128 if wide % 128 == 0 else wide

        def step(i, carry):
            cut = pl.ds(pl.multiple_of(s * wide + i * tile, tile), tile)
            blend = mom[:, cut] + grad[:, cut].astype(F32)
            high[:, cut], low[:, cut] = split(blend)
            high_t[cut, :], low_t[cut, :] = split(blend.T)
            return carry

        lax.fori_loop(0, wide // tile, step, 0)

    gather(at, one, right, prepare)
    for s in range(at.hz + at.hx + 1, cuts):
        prepare(s)

    total = jnp.zeros((rows, 2 * rank), F32)
    for i in range(cuts):
        cut = pl.ds(i * wide, wide)
        piece = right[pl.ds(i * nz // cuts, nz // cuts)].reshape(wide, rank)
        high_r, low_r = split(piece)
        pair = jnp.concatenate([high_r, low_r], axis=1)
        total = total + dot(high[:, cut], pair, ((1,), (0,)))
        total = total + dot(low[:, cut], pair, ((1,), (0,)))
    part[...] = total[:, :rank] + total[:, rank:]
    for o in range(1, ny):
        to = at.yr(o)
        misc.send(("ysum", o), part.at[pl.ds(to * share, share)], yrecv.at[o - 1], at.to(oy=o))
    mine = pl.ds(y * share, share)
    own_rows = part[mine]
    for o in range(1, ny):
        misc.got(("ysum", o), yrecv.at[o - 1], own)
        own_rows = own_rows + yrecv[o - 1]
    proj[mine] = own_rows
    for o in range(1, ny):
        misc.send(("yall", o), proj.at[mine], proj.at[mine], at.to(oy=o))
    for o in range(1, ny):
        theirs = pl.ds(at.yr(-o) * share, share)
        misc.got(("yall", o), proj.at[theirs], own)

    projected = proj[...]
    gram[...] = dot(projected, projected, ((0,), (0,)), HIGHEST)
    bit = rank // (2 * ny)
    my_bit = pl.ds((y * 2 + c) * bit, bit)
    misc.send("gsib", gram.at[pl.ds((y * 2 + 1 - c) * bit, bit)], graw.at[0], at.to(oc=1))
    high_p, low_p = split(projected)
    pair_p = jnp.concatenate([high_p, low_p], axis=1)
    block = columns // nz

    def make(o):
        cut = pl.ds(pl.multiple_of(at.zr(o) * block, 32), block)
        both = dot(high_t[cut], pair_p, ((1,), (0,))) + dot(low_t[cut], pair_p, ((1,), (0,)))
        parts[o] = (both[:, :rank] + both[:, rank:]).reshape(nx, 2, depth, rank)

    spread = [(oy, oc) for oy in range(ny) for oc in range(2) if (oy, oc) != (0, 0)]

    def gram_steps(s):
        if s == 0:
            misc.got("gsib", graw.at[0], own)
            graw[1] = graw[0] + gram[my_bit]
            for o in range(1, nx):
                misc.send(("gx", o), graw.at[1], gx.at[o - 1], at.to(ox=o))
        if s == 1:
            total = graw[1]
            for o in range(1, nx):
                misc.got(("gx", o), gx.at[o - 1], own)
                total = total + gx[o - 1]
            graw[2] = total
            for o in range(1, nz):
                misc.send(("gz", o), graw.at[2], gz.at[o - 1], at.to(oz=o))
        if s == 2:
            total = graw[2]
            for o in range(1, nz):
                misc.got(("gz", o), gz.at[o - 1], own)
                total = total + gz[o - 1]
            gall[my_bit] = total
            for oy, oc in spread:
                misc.send(("gall", oy, oc), gall.at[my_bit], gall.at[my_bit], at.to(oy=oy, oc=oc))
        if s == 3 or s == at.hz + at.hx and s < 3:
            for oy, oc in spread:
                theirs = pl.ds((at.yr(-oy) * 2 + (c + oc) % 2) * bit, bit)
                misc.got(("gall", oy, oc), gall.at[theirs], own)
            work[:, pl.ds(0, rank)] = gall[...]
            row = lax.broadcasted_iota(jnp.int32, (rank, rank), 0)
            col = lax.broadcasted_iota(jnp.int32, (rank, rank), 1)
            work[:, pl.ds(rank, rank)] = jnp.where(row == col, 1.0, 0.0).astype(F32)

    blocks = rank // ROWS
    state = {"next": 0}

    def invert(count):
        start = state["next"]
        stop = min(blocks, start + count)
        state["next"] = stop
        if stop > start:

            def step(b, carry):
                invert_block(b, work, inv)
                return carry

            lax.fori_loop(start, stop, step, 0)

    def beside_reduce(s):
        for step in range(4):
            if min(step, at.hz + at.hx) == s:
                gram_steps(step)
        if s >= 4:
            invert(2)

    b_sum, a_sum = reduce(at, two, parts, sib, xb, zsum, zb, za, xsum, xa, make, beside_reduce)
    whole[z, x, c, pl.ds(0, FIRST)] = b_sum
    whole[z, x, c, pl.ds(FIRST, depth - FIRST)] = a_sum
    gather(at, three, whole, lambda s: invert(2))
    invert(blocks)

    high_i, low_i = split(inv[...])
    pair_i = jnp.concatenate([high_i, low_i], axis=0)

    def couple(value):
        high_v, low_v = split(value)
        both = dot(high_v, pair_i, ((1,), (1,))) + dot(low_v, pair_i, ((1,), (1,)))
        return both[:, :rank] + both[:, rank:]

    def couple_block(i, squares):
        coupled = couple(whole[i].reshape(block, rank))
        coupled_ref[pl.ds(pl.multiple_of(i * block, 32), block), :] = coupled.astype(BF16)
        return squares + jnp.sum((coupled * coupled).reshape(block // 8, 8, rank), axis=0)

    sq[0] = lax.fori_loop(0, nz, couple_block, jnp.zeros((8, rank), F32))
    for o in range(1, ny):
        misc.send(("sq", o), sq.at[0], sq.at[o], at.to(oy=o))
    left_ref[...] = dot(projected, inv[...], ((1,), (1,)), HIGHEST)
    mine_coupled = couple(whole[z, x, c])
    squares = sq[0]
    for o in range(1, ny):
        misc.got(("sq", o), sq.at[o], own)
        squares = squares + sq[o]
    squares = jnp.sum(squares, axis=0, keepdims=True)
    right_ref[...] = mine_coupled * lax.rsqrt(squares + 1e-06)
    for wire in (one, two, three, misc):
        wire.drain()


def update(left, coupled, momentum, gradient, out):
    change = dot(left[...].astype(BF16), coupled[...], ((1,), (1,)))
    out[...] = momentum[...] + gradient[...].astype(F32) - 0.05 * change


def local(nz, nx, ny, momentum, gradient, right_prev):
    rows, columns = momentum.shape
    depth, rank = right_prev.shape
    cuts = 4 if columns % 512 == 0 and nz % 4 == 0 else 1
    hz, hx = nz // 2, nx // 2
    rest = depth - FIRST
    bit = rank // (2 * ny)
    steps = 4 * hz + 2 * hx + 2 * hx * nz + nz
    few = 2 * (ny - 1) + 1 + (nx - 1) + (nz - 1) + (2 * ny - 1) + (ny - 1)
    vmem = pltpu.VMEM
    sems = []
    for count in (steps, steps, steps, few):
        sems += [pltpu.SemaphoreType.DMA((count,)), pltpu.SemaphoreType.DMA((count,))]
    left_factor, right_factor, coupled = pl.pallas_call(
        functools.partial(factors, nz, nx, ny, cuts),
        out_shape=(
            jax.ShapeDtypeStruct((rows, rank), F32),
            jax.ShapeDtypeStruct((depth, rank), F32),
            jax.ShapeDtypeStruct((columns, rank), BF16),
        ),
        in_specs=[
            pl.BlockSpec(memory_space=pl.ANY),
            pl.BlockSpec(memory_space=pl.ANY),
            pl.BlockSpec(memory_space=vmem),
        ],
        out_specs=(pl.BlockSpec(memory_space=vmem),) * 3,
        scratch_shapes=[
            vmem((rows, columns), F32),
            vmem((rows, columns), BF16),
            vmem((rows, columns), BF16),
            vmem((rows, columns), BF16),
            vmem((columns, rows), BF16),
            vmem((columns, rows), BF16),
            vmem((nz, nx, 2, depth, rank), F32),
            vmem((nz, nx, 2, depth, rank), F32),
            vmem((nz, nx, depth, rank), F32),
            vmem((nz, 2, hx, FIRST, rank), F32),
            vmem((nz, FIRST, rank), F32),
            vmem((2, hz, FIRST, rank), F32),
            vmem((2, hz, nx, rest, rank), F32),
            vmem((nx, rest, rank), F32),
            vmem((2, hx, rest, rank), F32),
            vmem((nz, nx, 2, depth, rank), F32),
            vmem((rows, rank), F32),
            vmem((rows, rank), F32),
            vmem((ny - 1, rows // ny, rank), F32),
            vmem((rank, rank), F32),
            vmem((rank, 2 * rank), F32),
            vmem((rank, rank), F32),
            vmem((3, bit, rank), F32),
            vmem((nx - 1, bit, rank), F32),
            vmem((nz - 1, bit, rank), F32),
            vmem((rank, rank), F32),
            vmem((ny, 8, rank), F32),
            pltpu.SemaphoreType.DMA((2, cuts)),
            *sems,
        ],
        compiler_params=pltpu.CompilerParams(
            collective_id=0, has_side_effects=True, vmem_limit_bytes=56 * 1024 * 1024
        ),
    )(momentum, gradient, right_prev)

    tile = 512 if columns % 512 == 0 else columns
    new_momentum = pl.pallas_call(
        update,
        out_shape=jax.ShapeDtypeStruct((rows, columns), F32),
        grid=(columns // tile,),
        in_specs=[
            pl.BlockSpec((rows, rank), lambda i: (0, 0)),
            pl.BlockSpec((tile, rank), lambda i: (i, 0)),
            pl.BlockSpec((rows, tile), lambda i: (0, i)),
            pl.BlockSpec((rows, tile), lambda i: (0, i)),
        ],
        out_specs=pl.BlockSpec((rows, tile), lambda i: (0, i)),
        compiler_params=pltpu.CompilerParams(vmem_limit_bytes=32 * 1024 * 1024),
    )(left_factor, coupled, momentum, gradient)
    return (new_momentum, left_factor, right_factor)


def solution(mesh):
    ny = mesh.shape["tensor"]
    nx = min(4, mesh.shape["dp"] // 4)
    nz = mesh.shape["dp"] // (2 * nx)
    return jax.shard_map(
        functools.partial(local, nz, nx, ny),
        mesh=mesh,
        in_specs=(P("dp", "tensor"), P("dp", "tensor"), P(("tensor", "dp"), None)),
        out_specs=(P("dp", "tensor"), P("dp", None), P(("tensor", "dp"), None)),
        check_vma=False,
    )
```

```python
import functools

import jax
import jax.numpy as jnp
from jax import lax
from jax.experimental import pallas as pl
from jax.experimental.pallas import tpu as pltpu
from jax.sharding import PartitionSpec as P

HIGHEST = lax.Precision.HIGHEST
MESH = pl.DeviceIdType.MESH
F32 = jnp.float32
BF16 = jnp.bfloat16
ROWS = 8
FIRST = 80
SIGNS = (1, -1)


def dot(a, b, dims, precision=None):
    return lax.dot_general(a, b, (dims, ((), ())), precision=precision, preferred_element_type=F32)


def split(value):
    high = value.astype(BF16)
    return high, (value - high.astype(F32)).astype(BF16)


class Place:
    def __init__(self, nz, nx, ny):
        self.nz, self.nx, self.ny = nz, nx, ny
        at = lax.axis_index("dp")
        self.y = lax.axis_index("tensor")
        self.z, self.x, self.c = at // (2 * nx), (at // 2) % nx, at % 2

    def zr(self, o):
        return (self.z + (o + 2 * self.nz)) % self.nz

    def xr(self, o):
        return (self.x + (o + 2 * self.nx)) % self.nx

    def yr(self, o):
        return (self.y + (o + 2 * self.ny)) % self.ny

    def to(self, oz=0, ox=0, oy=0, oc=0):
        core = (self.c + oc) % 2
        return ((self.zr(oz) * self.nx + self.xr(ox)) * 2 + core, self.yr(oy))

    def partners(self):
        out = [dict(oc=1)]
        out += [dict(ox=o) for o in range(1, self.nx)]
        out += [dict(oz=o) for o in range(1, self.nz)]
        out += [dict(oy=o, oc=k) for o in range(1, self.ny) for k in range(2)]
        return out


class Wire:
    def __init__(self, send_sems, recv_sems):
        self.sems, self.names, self.sent = (send_sems, recv_sems), {}, []

    def copy(self, name, src, dst, device):
        at = self.names.setdefault(name, len(self.names))
        return pltpu.make_async_remote_copy(
            src_ref=src,
            dst_ref=dst,
            send_sem=self.sems[0].at[at],
            recv_sem=self.sems[1].at[at],
            device_id=device,
            device_id_type=MESH,
        )

    def send(self, name, src, dst, device):
        copy = self.copy(name, src, dst, device)
        copy.start()
        self.sent.append(copy)

    def got(self, name, dst, device):
        self.copy(name, dst, dst, device).wait_recv()

    def drain(self):
        for copy in self.sent:
            copy.wait_send()
        self.sent = []


def first_rows(d, half):
    if not half:
        return pl.ds(0, FIRST)
    return pl.ds(0 if d > 0 else FIRST // 2, FIRST // 2)


def some_x(d, half, nx):
    if not half:
        return pl.ds(0, nx)
    return pl.ds(0 if d > 0 else nx // 2, nx // 2)


def gather(at, wire, buf, hook, pair):
    nz, nx, z, x, c, zr, xr = at.nz, at.nx, at.z, at.x, at.c, at.zr, at.xr
    depth = buf.shape[3]
    rest = pl.ds(FIRST, depth - FIRST)
    own = at.to()

    def send(name, ref, **where):
        wire.send(name, ref, ref, at.to(**where))

    def got(name, ref):
        wire.got(name, ref, own)

    def turn(o, e, t):
        return buf.at[zr(o), xr(-e * t), c, first_rows(e, t == 2)]

    def across(o):
        for e in SIGNS:
            send(("bx", o, e, 1), buf.at[zr(o), x, c, first_rows(e, False)], ox=e)

    def pass_on(o):
        for e in SIGNS:
            got(("bx", o, e, 1), turn(o, e, 1))
            send(("bx", o, e, 2), buf.at[zr(o), xr(-e), c, first_rows(e, True)], ox=e)

    def close(o):
        for e in SIGNS:
            got(("bx", o, e, 2), turn(o, e, 2))
        send(("both", o), buf.at[zr(o), :, c], oc=1)

    def other(o):
        got(("both", o), buf.at[zr(o), :, 1 - c])

    for d in SIGNS:
        for k in (2, 1):
            send(("bz", d, k), buf.at[z, x, c, first_rows(d, False)], oz=d * k)
    for o in (2, 1, 3):
        send(("ax", o), buf.at[z, x, c, rest], ox=o)
    across(0)
    hook(0)
    for d in SIGNS:
        got(("bz", d, 1), buf.at[zr(-d), x, c, first_rows(d, False)])
        across(-d % nz)
    for d in SIGNS:
        got(("bz", d, 2), buf.at[zr(-2 * d), x, c, first_rows(d, False)])
        send(("bz", d, 4), buf.at[zr(-2 * d), x, c, first_rows(d, True)], oz=2 * d)
        send(("bz", d, 3), buf.at[zr(-2 * d), x, c, first_rows(d, False)], oz=d)
    pass_on(0)
    for o in (1, 3, 2):
        got(("ax", o), buf.at[z, xr(-o), c, rest])
    for d in SIGNS:
        for k in (2, 1):
            send(("az", d, k), buf.at[z, :, c, rest], oz=d * k)
    for d in SIGNS:
        across(-2 * d % nz)
    hook(1)
    for d in SIGNS:
        pass_on(-d % nz)
    for d in SIGNS:
        got(("bz", d, 3), buf.at[zr(-3 * d), x, c, first_rows(d, False)])
        across(-3 * d % nz)
    for d in SIGNS:
        got(("az", d, 2), buf.at[zr(-2 * d), :, c, rest])
        send(("az", d, 4), buf.at[zr(-2 * d), some_x(d, True, nx), c, rest], oz=2 * d)
        send(("az", d, 3), buf.at[zr(-2 * d), :, c, rest], oz=d)
    for d in SIGNS:
        got(("bz", d, 4), buf.at[zr(-4 * d), x, c, first_rows(d, True)])
    across(4)
    for d in SIGNS:
        pass_on(-2 * d % nz)
    close(0)
    hook(2)
    for d in SIGNS:
        got(("az", d, 1), buf.at[zr(-d), :, c, rest])
        close(-d % nz)
    for d in SIGNS:
        pass_on(-3 * d % nz)
    hook(3)
    pass_on(4)
    other(0)
    for d in SIGNS:
        other(-d % nz)
    pair(1)
    for d in SIGNS:
        close(-2 * d % nz)
    for d in SIGNS:
        got(("az", d, 3), buf.at[zr(-3 * d), :, c, rest])
        close(-3 * d % nz)
    for d in SIGNS:
        other(-2 * d % nz)
    pair(2)
    for d in SIGNS:
        got(("az", d, 4), buf.at[zr(-4 * d), some_x(d, True, nx), c, rest])
    close(4)
    for d in SIGNS:
        other(-3 * d % nz)
    pair(3)
    other(4)
    pair(4)


def reduce(at, wire, parts, sib, xb, zsum, zb, za, xsum, xa, make, hook):
    nz, nx, x, c, xr = at.nz, at.nx, at.x, at.c, at.xr
    depth = parts.shape[3]
    rest = pl.ds(FIRST, depth - FIRST)
    own = at.to()

    def term(o):
        make(o)
        wire.send(("both", o), parts.at[o, :, 1 - c], sib.at[o], at.to(oc=1))

    def combine(o):
        wire.got(("both", o), sib.at[o], own)
        parts[o, :, c] = parts[o, :, c] + sib[o]
        for i, e in enumerate(SIGNS):
            rows = first_rows(e, True)
            wire.send(("bx", o, e, 1), parts.at[o, xr(2), c, rows], xb.at[o, i, 0, rows], at.to(ox=e))

    def pass_on(o):
        for i, e in enumerate(SIGNS):
            rows = first_rows(e, True)
            wire.got(("bx", o, e, 1), xb.at[o, i, 0, rows], own)
            parts[o, xr(e), c, rows] = parts[o, xr(e), c, rows] + xb[o, i, 0, rows]
            rows = first_rows(e, False)
            wire.send(("bx", o, e, 2), parts.at[o, xr(e), c, rows], xb.at[o, i, 1], at.to(ox=e))

    def close(o):
        for i, e in enumerate(SIGNS):
            wire.got(("bx", o, e, 2), xb.at[o, i, 1], own)
        zsum[o] = parts[o, x, c, pl.ds(0, FIRST)] + xb[o, 0, 1] + xb[o, 1, 1]

    def send_a(i, d, k):
        xs = some_x(d, k == 4, nx)
        wire.send(("az", d, k), parts.at[d * k % nz, xs, c, rest], za.at[i, k - 1, xs], at.to(oz=d * (1, 2, 1, 2)[k - 1]))

    def got_a(i, d, k):
        xs = some_x(d, k == 4, nx)
        wire.got(("az", d, k), za.at[i, k - 1, xs], own)
        return xs

    def send_b(i, d, k):
        rows = first_rows(d, k == 4)
        wire.send(("bz", d, k), zsum.at[d * k % nz, rows], zb.at[i, k - 1, rows], at.to(oz=d * (1, 2, 1, 2)[k - 1]))

    def got_b(i, d, k):
        rows = first_rows(d, k == 4)
        wire.got(("bz", d, k), zb.at[i, k - 1, rows], own)
        return rows

    two = tuple(enumerate(SIGNS))
    term(4)
    term(3)
    term(5)
    combine(4)
    for i, d in two:
        send_a(i, d, 4)
    term(2)
    for o in (3, 5):
        combine(o)
    for i, d in two:
        send_a(i, d, 3)
    term(6)
    hook(0)
    pass_on(4)
    term(1)
    for o in (2, 6):
        combine(o)
    for o in (3, 5):
        pass_on(o)
    term(7)
    hook(1)
    for i, d in two:
        o = 2 * d % nz
        for k in (3, 4):
            xs = got_a(i, d, k)
            parts[o, xs, c, rest] = parts[o, xs, c, rest] + za[i, k - 1, xs]
        send_a(i, d, 2)
    close(4)
    for i, d in two:
        send_b(i, d, 4)
    for o in (1, 7):
        combine(o)
    for i, d in two:
        send_a(i, d, 1)
    for o in (2, 6):
        pass_on(o)
    term(0)
    for o in (3, 5):
        close(o)
    for i, d in two:
        send_b(i, d, 3)
    hook(2)
    combine(0)
    for o in (1, 7):
        pass_on(o)
    xsum[...] = parts[0, :, c, rest]
    for i, d in two:
        for k in (1, 2):
            got_a(i, d, k)
            xsum[...] = xsum[...] + za[i, k - 1]
    for o in range(1, nx):
        wire.send(("ax", o), xsum.at[xr(o)], xa.at[o - 1], at.to(ox=o))
    for o in (2, 6):
        close(o)
    for i, d in two:
        o = 2 * d % nz
        for k in (3, 4):
            rows = got_b(i, d, k)
            zsum[o, rows] = zsum[o, rows] + zb[i, k - 1, rows]
        send_b(i, d, 2)
    pass_on(0)
    hook(3)
    for o in (1, 7):
        close(o)
    for i, d in two:
        send_b(i, d, 1)
    hook(4)
    close(0)
    last = xsum[x]
    for o in range(1, nx):
        wire.got(("ax", o), xa.at[o - 1], own)
        last = last + xa[o - 1]
    first = zsum[0]
    for i, d in two:
        for k in (2, 1):
            got_b(i, d, k)
            first = first + zb[i, k - 1]
    return first, last


def invert_block(b, work, out_ref):
    size = out_ref.shape[0]
    start = pl.multiple_of(b * ROWS, ROWS)
    panel = work[pl.ds(start, ROWS), :]
    first = pltpu.roll(panel[:, :size], (size - start) % size, 1)
    g = {}
    for i in range(ROWS):
        for j in range(i, ROWS):
            g[i, j] = jnp.broadcast_to(first[i : i + 1, j : j + 1], (1, size))
    scale = []
    for k in range(ROWS):
        r = lax.rsqrt(g[k, k])
        scale.append(r)
        for j in range(k + 1, ROWS):
            g[k, j] = g[k, j] * r
        for i in range(k + 1, ROWS):
            for j in range(i, ROWS):
                g[i, j] = g[i, j] - g[k, i] * g[k, j]
    done = []
    for i in range(ROWS):
        left, right = panel[i : i + 1, :size], panel[i : i + 1, size:]
        for k in range(i):
            left = left - g[k, i] * done[k][0]
            right = right - g[k, i] * done[k][1]
        done.append((left * scale[i], right * scale[i]))
    upper = jnp.concatenate([d[0] for d in done], axis=0)
    inverse = jnp.concatenate([d[1] for d in done], axis=0)
    out_ref[pl.ds(start, ROWS), :] = inverse
    both = jnp.concatenate([upper, inverse], axis=1)
    work[...] = work[...] - dot(upper, both, ((0,), (0,)), HIGHEST)


def factors(
    nz, nx, ny,
    momentum, gradient, right_prev,
    new_ref, left_ref, right_ref,
    blend, grad, high, low, high_t, low_t, right, parts, sib, xb, zsum, zb, za, xsum, xa, whole,
    acc, part, proj, yrecv, gram, work, inv, graw, gx, gz, gall, sq,
    load_sem, s1, r1, s2, r2, s3, r3, s4, r4,
):
    at = Place(nz, nx, ny)
    z, x, c, y = at.z, at.x, at.c, at.y
    own = at.to()
    rows, columns = blend.shape
    rank = proj.shape[1]
    cuts = nz // 2
    wide = columns // cuts
    block = columns // nz
    depth = right_prev.shape[0]
    share = rows // ny
    one, two, three, misc = Wire(s1, r1), Wire(s2, r2), Wire(s3, r3), Wire(s4, r4)

    loads = []
    for i in range(cuts):
        cut = pl.ds(i * wide, wide)
        for j, (src, dst) in enumerate(((momentum, blend), (gradient, grad))):
            copy = pltpu.make_async_copy(src.at[:, cut], dst.at[:, cut], load_sem.at[j, i])
            copy.start()
            loads.append(copy)

    partners = at.partners()
    barrier = pltpu.get_barrier_semaphore()
    for where in partners:
        pl.semaphore_signal(barrier, inc=1, device_id=at.to(**where), device_id_type=MESH)
    right[z, x, c] = right_prev[...]

    def prepare(s):
        loads[2 * s].wait()
        loads[2 * s + 1].wait()

        def step(i, carry):
            cut = pl.ds(pl.multiple_of(s * wide + i * 128, 128), 128)
            value = blend[:, cut] + grad[:, cut].astype(F32)
            blend[:, cut] = value
            high[:, cut], low[:, cut] = split(value)
            high_t[cut, :], low_t[cut, :] = split(value.T)
            return carry

        lax.fori_loop(0, wide // 128, step, 0)

    for i in range(cuts - 1):
        prepare(i)
    pl.semaphore_wait(barrier, len(partners))

    def pair_at(k):
        sign = 1 - 2 * ((z + 1) % 2)
        move = (0, sign, -sign, 2)[k - 1]
        return (z // 2 + move + cuts) % cuts

    def project(k):
        p = pair_at(k)
        cut = pl.ds(pl.multiple_of(p * wide, 128), wide)
        high_r, low_r = split(right[pl.ds(2 * p, 2)].reshape(wide, rank))
        both = jnp.concatenate([high_r, low_r], axis=1)
        more = dot(high[:, cut], both, ((1,), (0,))) + dot(low[:, cut], both, ((1,), (0,)))
        acc[...] = more if k == 1 else acc[...] + more

    def prepare_last(s):
        if s == 0:
            prepare(cuts - 1)

    gather(at, one, right, prepare_last, project)

    part[...] = acc[:, pl.ds(0, rank)] + acc[:, pl.ds(rank, rank)]
    for o in (2, 1, 3):
        to = at.yr(o)
        misc.send(("ysum", o), part.at[pl.ds(to * share, share)], yrecv.at[o - 1], at.to(oy=o))
    mine = pl.ds(y * share, share)
    own_rows = part[mine]
    for o in range(1, ny):
        misc.got(("ysum", o), yrecv.at[o - 1], own)
        own_rows = own_rows + yrecv[o - 1]
    proj[mine] = own_rows
    for o in (2, 1, 3):
        misc.send(("yall", o), proj.at[mine], proj.at[mine], at.to(oy=o))
    for o in range(1, ny):
        theirs = pl.ds(at.yr(-o) * share, share)
        misc.got(("yall", o), proj.at[theirs], own)

    projected = proj[...]
    gram[...] = dot(projected, projected, ((0,), (0,)), HIGHEST)
    bit = rank // (2 * ny)
    my_bit = pl.ds((y * 2 + c) * bit, bit)
    misc.send("gsib", gram.at[pl.ds((y * 2 + 1 - c) * bit, bit)], graw.at[0], at.to(oc=1))
    high_p, low_p = split(projected)
    pair_p = jnp.concatenate([high_p, low_p], axis=1)

    def make(o):
        cut = pl.ds(pl.multiple_of(at.zr(o) * block, 32), block)
        both = dot(high_t[cut], pair_p, ((1,), (0,))) + dot(low_t[cut], pair_p, ((1,), (0,)))
        parts[o] = (both[:, :rank] + both[:, rank:]).reshape(nx, 2, depth, rank)

    spread = [(oy, oc) for oy in range(ny) for oc in range(2) if (oy, oc) != (0, 0)]

    def gram_steps(s):
        if s == 0:
            misc.got("gsib", graw.at[0], own)
            graw[1] = graw[0] + gram[my_bit]
            for o in range(1, nx):
                misc.send(("gx", o), graw.at[1], gx.at[o - 1], at.to(ox=o))
        if s == 1:
            total = graw[1]
            for o in range(1, nx):
                misc.got(("gx", o), gx.at[o - 1], own)
                total = total + gx[o - 1]
            graw[2] = total
            for o in (4, 3, 5, 2, 6, 1, 7):
                misc.send(("gz", o), graw.at[2], gz.at[o - 1], at.to(oz=o))
        if s == 2:
            total = graw[2]
            for o in range(1, nz):
                misc.got(("gz", o), gz.at[o - 1], own)
                total = total + gz[o - 1]
            gall[my_bit] = total
            for oy, oc in spread:
                misc.send(("gall", oy, oc), gall.at[my_bit], gall.at[my_bit], at.to(oy=oy, oc=oc))
        if s == 3:
            for oy, oc in spread:
                theirs = pl.ds((at.yr(-oy) * 2 + (c + oc) % 2) * bit, bit)
                misc.got(("gall", oy, oc), gall.at[theirs], own)
            work[:, pl.ds(0, rank)] = gall[...]
            row = lax.broadcasted_iota(jnp.int32, (rank, rank), 0)
            col = lax.broadcasted_iota(jnp.int32, (rank, rank), 1)
            work[:, pl.ds(rank, rank)] = jnp.where(row == col, 1.0, 0.0).astype(F32)

    blocks = rank // ROWS
    state = {"next": 0}

    def invert(count):
        start = state["next"]
        stop = min(blocks, start + count)
        state["next"] = stop
        if stop > start:

            def step(b, carry):
                invert_block(b, work, inv)
                return carry

            lax.fori_loop(start, stop, step, 0)

    def beside_reduce(s):
        gram_steps(s)
        if s == 3:
            invert(3)
        if s == 4:
            invert(3)

    b_sum, a_sum = reduce(at, two, parts, sib, xb, zsum, zb, za, xsum, xa, make, beside_reduce)
    whole[z, x, c, pl.ds(0, FIRST)] = b_sum
    whole[z, x, c, pl.ds(FIRST, depth - FIRST)] = a_sum
    kept = {}

    def couple(value):
        high_v, low_v = split(value)
        both = dot(high_v, kept["inv"], ((1,), (1,))) + dot(low_v, kept["inv"], ((1,), (1,)))
        return both[:, :rank] + both[:, rank:]

    def beside_gather(s):
        invert((4, 2, 2, 2)[s])
        if s == 3:
            high_i, low_i = split(inv[...])
            kept["inv"] = jnp.concatenate([high_i, low_i], axis=0)
            left = dot(projected, inv[...], ((1,), (1,)), HIGHEST)
            left_ref[...] = left
            kept["left"] = (-0.05 * left).astype(BF16)

    def update(k):
        p = pair_at(k)
        cut = pl.ds(pl.multiple_of(p * wide, 128), wide)
        coupled = couple(whole[pl.ds(2 * p, 2)].reshape(wide, rank))
        squares = jnp.sum((coupled * coupled).reshape(wide // 8, 8, rank), axis=0)
        sq[0] = squares if k == 1 else sq[0] + squares
        if k == cuts:
            for o in (2, 1, 3):
                misc.send(("sq", o), sq.at[0], sq.at[o], at.to(oy=o))
        new_ref[:, cut] = blend[:, cut] + dot(kept["left"], coupled.astype(BF16), ((1,), (1,)))

    gather(at, three, whole, beside_gather, update)
    mine_coupled = couple(whole[z, x, c])
    squares = sq[0]
    for o in range(1, ny):
        misc.got(("sq", o), sq.at[o], own)
        squares = squares + sq[o]
    squares = jnp.sum(squares, axis=0, keepdims=True)
    right_ref[...] = mine_coupled * lax.rsqrt(squares + 1e-06)
    for wire in (one, two, three, misc):
        wire.drain()


def local(nz, nx, ny, momentum, gradient, right_prev):
    rows, columns = momentum.shape
    depth, rank = right_prev.shape
    rest = depth - FIRST
    bit = rank // (2 * ny)
    steps = 8 + (nx - 1) + 4 * nz + 8 + nz
    few = 2 * (ny - 1) + 1 + (nx - 1) + (nz - 1) + (2 * ny - 1) + (ny - 1)
    vmem = pltpu.VMEM
    sems = []
    for count in (steps, steps, steps, few):
        sems += [pltpu.SemaphoreType.DMA((count,)), pltpu.SemaphoreType.DMA((count,))]
    return pl.pallas_call(
        functools.partial(factors, nz, nx, ny),
        out_shape=(vmem((rows, columns), F32), vmem((rows, rank), F32), vmem((depth, rank), F32)),
        in_specs=[
            pl.BlockSpec(memory_space=pl.ANY),
            pl.BlockSpec(memory_space=pl.ANY),
            pl.BlockSpec(memory_space=vmem),
        ],
        out_specs=(pl.BlockSpec(memory_space=vmem),) * 3,
        scratch_shapes=[
            vmem((rows, columns), F32),
            vmem((rows, columns), BF16),
            vmem((rows, columns), BF16),
            vmem((rows, columns), BF16),
            vmem((columns, rows), BF16),
            vmem((columns, rows), BF16),
            vmem((nz, nx, 2, depth, rank), F32),
            vmem((nz, nx, 2, depth, rank), F32),
            vmem((nz, nx, depth, rank), F32),
            vmem((nz, 2, 2, FIRST, rank), F32),
            vmem((nz, FIRST, rank), F32),
            vmem((2, 4, FIRST, rank), F32),
            vmem((2, 4, nx, rest, rank), F32),
            vmem((nx, rest, rank), F32),
            vmem((nx - 1, rest, rank), F32),
            vmem((nz, nx, 2, depth, rank), F32),
            vmem((rows, 2 * rank), F32),
            vmem((rows, rank), F32),
            vmem((rows, rank), F32),
            vmem((ny - 1, rows // ny, rank), F32),
            vmem((rank, rank), F32),
            vmem((rank, 2 * rank), F32),
            vmem((rank, rank), F32),
            vmem((3, bit, rank), F32),
            vmem((nx - 1, bit, rank), F32),
            vmem((nz - 1, bit, rank), F32),
            vmem((rank, rank), F32),
            vmem((ny, 8, rank), F32),
            pltpu.SemaphoreType.DMA((2, nz // 2)),
            *sems,
        ],
        compiler_params=pltpu.CompilerParams(
            collective_id=0, has_side_effects=True, vmem_limit_bytes=48 * 1024 * 1024
        ),
    )(momentum, gradient, right_prev)


def solution(mesh):
    ny = mesh.shape["tensor"]
    nx = 4
    nz = mesh.shape["dp"] // (2 * nx)
    return jax.shard_map(
        functools.partial(local, nz, nx, ny),
        mesh=mesh,
        in_specs=(P("dp", "tensor"), P("dp", "tensor"), P(("tensor", "dp"), None)),
        out_specs=(P("dp", "tensor"), P("dp", None), P(("tensor", "dp"), None)),
        check_vma=False,
    )
```

```python
import functools

import jax
import jax.numpy as jnp
from jax import lax
from jax.experimental import pallas as pl
from jax.experimental.pallas import tpu as pltpu
from jax.sharding import PartitionSpec as P

HIGHEST = lax.Precision.HIGHEST
MESH = pl.DeviceIdType.MESH
F32 = jnp.float32
BF16 = jnp.bfloat16
ROWS = 8
FIRST = 72
SIGNS = (1, -1)


def dot(a, b, dims, precision=None):
    return lax.dot_general(a, b, (dims, ((), ())), precision=precision, preferred_element_type=F32)


def split(value):
    high = value.astype(BF16)
    return high, (value - high.astype(F32)).astype(BF16)


class Place:
    def __init__(self, nz, nx, ny):
        self.nz, self.nx, self.ny = nz, nx, ny
        at = lax.axis_index("dp")
        self.y = lax.axis_index("tensor")
        self.z, self.x, self.c = at // (2 * nx), (at // 2) % nx, at % 2

    def zr(self, o):
        return (self.z + (o + 2 * self.nz)) % self.nz

    def xr(self, o):
        return (self.x + (o + 2 * self.nx)) % self.nx

    def yr(self, o):
        return (self.y + (o + 2 * self.ny)) % self.ny

    def to(self, oz=0, ox=0, oy=0, oc=0):
        core = (self.c + oc) % 2
        return ((self.zr(oz) * self.nx + self.xr(ox)) * 2 + core, self.yr(oy))

    def partners(self):
        out = [dict(oc=1)]
        out += [dict(ox=o) for o in range(1, self.nx)]
        out += [dict(oz=o) for o in range(1, self.nz)]
        out += [dict(oy=o, oc=k) for o in range(1, self.ny) for k in range(2)]
        return out


class Wire:
    def __init__(self, send_sems, recv_sems):
        self.sems, self.names, self.sent = (send_sems, recv_sems), {}, []

    def copy(self, name, src, dst, device):
        at = self.names.setdefault(name, len(self.names))
        return pltpu.make_async_remote_copy(
            src_ref=src,
            dst_ref=dst,
            send_sem=self.sems[0].at[at],
            recv_sem=self.sems[1].at[at],
            device_id=device,
            device_id_type=MESH,
        )

    def send(self, name, src, dst, device):
        copy = self.copy(name, src, dst, device)
        copy.start()
        self.sent.append(copy)

    def got(self, name, dst, device):
        self.copy(name, dst, dst, device).wait_recv()

    def drain(self):
        for copy in self.sent:
            copy.wait_send()
        self.sent = []


def first_rows(d, half):
    if not half:
        return pl.ds(0, FIRST)
    cut = (FIRST // 16 + 1) * 8
    return pl.ds(0, cut) if d > 0 else pl.ds(cut, FIRST - cut)


def some_x(d, half, nx):
    if not half:
        return pl.ds(0, nx)
    return pl.ds(0 if d > 0 else nx // 2, nx // 2)


def gather(at, wire, buf, hook, pair):
    nz, nx, z, x, c, zr, xr = at.nz, at.nx, at.z, at.x, at.c, at.zr, at.xr
    depth = buf.shape[3]
    rest = pl.ds(FIRST, depth - FIRST)
    own = at.to()

    def send(name, ref, **where):
        wire.send(name, ref, ref, at.to(**where))

    def got(name, ref):
        wire.got(name, ref, own)

    def turn(o, e, t):
        return buf.at[zr(o), xr(-e * t), c, first_rows(e, t == 2)]

    def across(o):
        for e in SIGNS:
            send(("bx", o, e, 1), buf.at[zr(o), x, c, first_rows(e, False)], ox=e)

    def pass_on(o):
        for e in SIGNS:
            got(("bx", o, e, 1), turn(o, e, 1))
            send(("bx", o, e, 2), buf.at[zr(o), xr(-e), c, first_rows(e, True)], ox=e)

    def close(o):
        for e in SIGNS:
            got(("bx", o, e, 2), turn(o, e, 2))
        send(("both", o), buf.at[zr(o), :, c], oc=1)

    def other(o):
        got(("both", o), buf.at[zr(o), :, 1 - c])

    def group(d, k):
        if k < 4:
            return (0, 1, 3, 2)
        return (0, 1) if d > 0 else (3, 2)

    def straight(o):
        for j in (2, 1, 3):
            send(("bx", o, 0, j), buf.at[zr(o), x, c, first_rows(1, False)], ox=j)

    def spread(j):
        for d in SIGNS:
            for k in (2, 1):
                send(("az", d, k, j), buf.at[z, xr(-j), c, rest], oz=d * k)

    for d in SIGNS:
        for k in (2, 1):
            send(("bz", d, k), buf.at[z, x, c, first_rows(d, False)], oz=d * k)
    for o in (2, 1, 3):
        send(("ax", o), buf.at[z, x, c, rest], ox=o)
    across(0)
    spread(0)
    hook(0)
    for d in SIGNS:
        got(("bz", d, 1), buf.at[zr(-d), x, c, first_rows(d, False)])
        across(-d % nz)
    hook(1)
    for d in SIGNS:
        got(("bz", d, 2), buf.at[zr(-2 * d), x, c, first_rows(d, False)])
        send(("bz", d, 4), buf.at[zr(-2 * d), x, c, first_rows(d, True)], oz=2 * d)
        send(("bz", d, 3), buf.at[zr(-2 * d), x, c, first_rows(d, False)], oz=d)
    pass_on(0)
    for o in (1, 3, 2):
        got(("ax", o), buf.at[z, xr(-o), c, rest])
        spread(o)
    for d in SIGNS:
        across(-2 * d % nz)
    hook(2)
    for d in SIGNS:
        pass_on(-d % nz)
    hook(3)
    close(0)
    for d in SIGNS:
        got(("bz", d, 3), buf.at[zr(-3 * d), x, c, first_rows(d, False)])
        across(-3 * d % nz)
    for d in SIGNS:
        got(("bz", d, 4), buf.at[zr(-4 * d), x, c, first_rows(d, True)])
    straight(4)
    for j in (0, 1, 3, 2):
        for d in SIGNS:
            got(("az", d, 2, j), buf.at[zr(-2 * d), xr(-j), c, rest])
            if j in group(d, 4):
                send(("az", d, 4, j), buf.at[zr(-2 * d), xr(-j), c, rest], oz=2 * d)
            send(("az", d, 3, j), buf.at[zr(-2 * d), xr(-j), c, rest], oz=d)
    hook(4)
    for d in SIGNS:
        pass_on(-2 * d % nz)
    for d in SIGNS:
        for j in group(d, 1):
            got(("az", d, 1, j), buf.at[zr(-d), xr(-j), c, rest])
        close(-d % nz)
    hook(5)
    for d in SIGNS:
        pass_on(-3 * d % nz)
    for d in SIGNS:
        close(-2 * d % nz)
    other(0)
    for d in SIGNS:
        other(-d % nz)
    pair(1)
    for d in SIGNS:
        for j in group(d, 3):
            got(("az", d, 3, j), buf.at[zr(-3 * d), xr(-j), c, rest])
        close(-3 * d % nz)
    for d in SIGNS:
        for j in group(d, 4):
            got(("az", d, 4, j), buf.at[zr(-4 * d), xr(-j), c, rest])
    for j in (1, 3, 2):
        got(("bx", 4, 0, j), buf.at[zr(4), xr(-j), c, first_rows(1, False)])
    send(("both", 4), buf.at[zr(4), :, c], oc=1)
    for d in SIGNS:
        other(-2 * d % nz)
    pair(2)
    for d in SIGNS:
        other(-3 * d % nz)
    pair(3)
    other(4)
    pair(4)


def reduce(at, wire, parts, sib, xb, zsum, zb, za, xsum, xa, make, hook):
    nz, nx, x, c, xr = at.nz, at.nx, at.x, at.c, at.xr
    depth = parts.shape[3]
    rest = pl.ds(FIRST, depth - FIRST)
    own = at.to()

    def term(o):
        make(o)
        wire.send(("both", o), parts.at[o, :, 1 - c], sib.at[o], at.to(oc=1))

    def combine(o):
        wire.got(("both", o), sib.at[o], own)
        parts[o, :, c] = parts[o, :, c] + sib[o]
        for e in SIGNS:
            rows = first_rows(e, True)
            wire.send(("bx", o, e, 1), parts.at[o, xr(2), c, rows], xb.at[o, 2, rows], at.to(ox=e))

    def pass_on(o):
        for i, e in enumerate(SIGNS):
            rows = first_rows(e, True)
            wire.got(("bx", o, e, 1), xb.at[o, 2, rows], own)
            parts[o, xr(e), c, rows] = parts[o, xr(e), c, rows] + xb[o, 2, rows]
            rows = first_rows(e, False)
            wire.send(("bx", o, e, 2), parts.at[o, xr(e), c, rows], xb.at[o, i], at.to(ox=e))

    def close(o):
        total = parts[o, x, c, pl.ds(0, FIRST)]
        for i, e in enumerate(SIGNS):
            wire.got(("bx", o, e, 2), xb.at[o, i], own)
            total = total + xb[o, i]
        zsum[o] = total

    def send_a(i, d, k):
        xs = some_x(d, k == 4, nx)
        wire.send(("az", d, k), parts.at[d * k % nz, xs, c, rest], za.at[i, k - 1, xs], at.to(oz=d * (1, 2, 1, 2)[k - 1]))

    def got_a(i, d, k):
        xs = some_x(d, k == 4, nx)
        wire.got(("az", d, k), za.at[i, k - 1, xs], own)
        return xs

    def send_b(i, d, k):
        rows = first_rows(d, k == 4)
        wire.send(("bz", d, k), zsum.at[d * k % nz, rows], zb.at[i, k - 1, rows], at.to(oz=d * (1, 2, 1, 2)[k - 1]))

    def got_b(i, d, k):
        rows = first_rows(d, k == 4)
        wire.got(("bz", d, k), zb.at[i, k - 1, rows], own)
        return rows

    two = tuple(enumerate(SIGNS))
    term(4)
    term(3)
    combine(4)
    for i, d in two:
        send_a(i, d, 4)
    term(5)
    hook(0)
    combine(3)
    term(2)
    combine(5)
    for i, d in two:
        send_a(i, d, 3)
    term(6)
    pass_on(4)
    combine(2)
    term(1)
    combine(6)
    hook(1)
    for o in (3, 5):
        pass_on(o)
    term(7)
    combine(1)
    for i, d in two:
        o = 2 * d % nz
        for k in (3, 4):
            xs = got_a(i, d, k)
            parts[o, xs, c, rest] = parts[o, xs, c, rest] + za[i, k - 1, xs]
        send_a(i, d, 2)
    close(4)
    for i, d in two:
        send_b(i, d, 4)
    term(0)
    combine(7)
    for i, d in two:
        send_a(i, d, 1)
    for o in (2, 6):
        pass_on(o)
    combine(0)
    hook(2)
    for o in (3, 5):
        close(o)
    for i, d in two:
        send_b(i, d, 3)
    for o in (1, 7):
        pass_on(o)
    hook(3)
    for o in (2, 6):
        close(o)
    for i, d in two:
        o = 2 * d % nz
        for k in (4, 3):
            rows = got_b(i, d, k)
            zsum[o, rows] = zsum[o, rows] + zb[i, k - 1, rows]
        send_b(i, d, 2)
    pass_on(0)
    hook(4)
    for o in (1, 7):
        close(o)
    for i, d in two:
        send_b(i, d, 1)
    xsum[...] = parts[0, :, c, rest]
    for i, d in two:
        for k in (1, 2):
            got_a(i, d, k)
            xsum[...] = xsum[...] + za[i, k - 1]
    for o in range(1, nx):
        wire.send(("ax", o), xsum.at[xr(o)], xa.at[o - 1], at.to(ox=o))
    hook(5)
    close(0)
    last = xsum[x]
    for o in range(1, nx):
        wire.got(("ax", o), xa.at[o - 1], own)
        last = last + xa[o - 1]
    first = zsum[0]
    for i, d in two:
        for k in (2, 1):
            got_b(i, d, k)
            first = first + zb[i, k - 1]
    return first, last


def invert_block(b, work, out_ref):
    size = out_ref.shape[0]
    start = pl.multiple_of(b * ROWS, ROWS)
    panel = work[pl.ds(start, ROWS), :]
    first = pltpu.roll(panel[:, :size], (size - start) % size, 1)
    g = {}
    for i in range(ROWS):
        for j in range(i, ROWS):
            g[i, j] = jnp.broadcast_to(first[i : i + 1, j : j + 1], (1, size))
    scale = []
    for k in range(ROWS):
        r = lax.rsqrt(g[k, k])
        scale.append(r)
        for j in range(k + 1, ROWS):
            g[k, j] = g[k, j] * r
        for i in range(k + 1, ROWS):
            for j in range(i, ROWS):
                g[i, j] = g[i, j] - g[k, i] * g[k, j]
    done = []
    for i in range(ROWS):
        left, right = panel[i : i + 1, :size], panel[i : i + 1, size:]
        for k in range(i):
            left = left - g[k, i] * done[k][0]
            right = right - g[k, i] * done[k][1]
        done.append((left * scale[i], right * scale[i]))
    upper = jnp.concatenate([d[0] for d in done], axis=0)
    inverse = jnp.concatenate([d[1] for d in done], axis=0)
    out_ref[pl.ds(start, ROWS), :] = inverse
    both = jnp.concatenate([upper, inverse], axis=1)
    work[...] = work[...] - dot(upper, both, ((0,), (0,)), HIGHEST)


def factors(
    nz, nx, ny,
    momentum, gradient, right_prev,
    new_ref, left_ref, right_ref,
    blend, grad, high, low, high_t, low_t, right, parts, sib, xb, zsum, zb, za, xsum, xa, whole,
    acc, part, proj, yrecv, gram, work, inv, graw, gx, gz, gall, sq,
    load_sem, s1, r1, s2, r2, s3, r3, s4, r4,
):
    at = Place(nz, nx, ny)
    z, x, c, y = at.z, at.x, at.c, at.y
    own = at.to()
    rows, columns = blend.shape
    rank = proj.shape[1]
    cuts = nz // 2
    wide = columns // cuts
    block = columns // nz
    depth = right_prev.shape[0]
    share = rows // ny
    one, two, three, misc = Wire(s1, r1), Wire(s2, r2), Wire(s3, r3), Wire(s4, r4)

    first_load = pltpu.make_async_copy(right_prev, right.at[z, x, c], load_sem.at[2, 0])
    first_load.start()
    loads = []
    for i in range(cuts):
        cut = pl.ds(i * wide, wide)
        for j, (src, dst) in enumerate(((momentum, blend), (gradient, grad))):
            copy = pltpu.make_async_copy(src.at[:, cut], dst.at[:, cut], load_sem.at[j, i])
            copy.start()
            loads.append(copy)

    partners = at.partners()
    barrier = pltpu.get_barrier_semaphore()
    for where in partners:
        pl.semaphore_signal(barrier, inc=1, device_id=at.to(**where), device_id_type=MESH)

    def prepare(s, piece):
        if piece == 0:
            loads[2 * s].wait()
            loads[2 * s + 1].wait()
        tiles = wide // 128
        half = (tiles + 1) // 2

        def step(i, carry):
            cut = pl.ds(pl.multiple_of(s * wide + i * 128, 128), 128)
            value = blend[:, cut] + grad[:, cut].astype(F32)
            blend[:, cut] = value
            high[:, cut], low[:, cut] = split(value)
            high_t[cut, :], low_t[cut, :] = split(value.T)
            return carry

        lax.fori_loop(*((0, half), (half, tiles))[piece], step, 0)


    units = [(i, piece) for i in range(cuts) for piece in range(2)]
    prepare(*units.pop(0))
    first_load.wait()
    pl.semaphore_wait(barrier, len(partners))

    def pair_at(k):
        sign = 1 - 2 * ((z + 1) % 2)
        move = (0, sign, -sign, 2)[k - 1]
        return (z // 2 + move + cuts) % cuts

    def project(k):
        p = pair_at(k)
        cut = pl.ds(pl.multiple_of(p * wide, 128), wide)
        high_r, low_r = split(right[pl.ds(2 * p, 2)].reshape(wide, rank))
        both = jnp.concatenate([high_r, low_r], axis=1)
        more = dot(high[:, cut], both, ((1,), (0,))) + dot(low[:, cut], both, ((1,), (0,)))
        acc[...] = more if k == 1 else acc[...] + more

    def prepare_some(s):
        for _ in range((3, 1, 1, 1, 1, 0)[s]):
            prepare(*units.pop(0))

    gather(at, one, right, prepare_some, project)

    part[...] = acc[:, pl.ds(0, rank)] + acc[:, pl.ds(rank, rank)]
    for o in (2, 1, 3):
        to = at.yr(o)
        misc.send(("ysum", o), part.at[pl.ds(to * share, share)], yrecv.at[o - 1], at.to(oy=o))
    mine = pl.ds(y * share, share)
    own_rows = part[mine]
    for o in range(1, ny):
        misc.got(("ysum", o), yrecv.at[o - 1], own)
        own_rows = own_rows + yrecv[o - 1]
    proj[mine] = own_rows
    for o in (2, 1, 3):
        misc.send(("yall", o), proj.at[mine], proj.at[mine], at.to(oy=o))
    for o in range(1, ny):
        theirs = pl.ds(at.yr(-o) * share, share)
        misc.got(("yall", o), proj.at[theirs], own)

    projected = proj[...]
    gram[...] = dot(projected, projected, ((0,), (0,)), HIGHEST)
    bit = rank // (2 * ny)
    my_bit = pl.ds((y * 2 + c) * bit, bit)
    misc.send("gsib", gram.at[pl.ds((y * 2 + 1 - c) * bit, bit)], graw.at[0], at.to(oc=1))
    high_p, low_p = split(projected)
    pair_p = jnp.concatenate([high_p, low_p], axis=1)

    def make(o):
        cut = pl.ds(pl.multiple_of(at.zr(o) * block, 32), block)
        both = dot(high_t[cut], pair_p, ((1,), (0,))) + dot(low_t[cut], pair_p, ((1,), (0,)))
        parts[o] = (both[:, :rank] + both[:, rank:]).reshape(nx, 2, depth, rank)

    spread = [(oy, oc) for oy in range(ny) for oc in range(2) if (oy, oc) != (0, 0)]

    def gram_steps(s):
        if s == 0:
            misc.got("gsib", graw.at[0], own)
            graw[1] = graw[0] + gram[my_bit]
            for o in range(1, nx):
                misc.send(("gx", o), graw.at[1], gx.at[o - 1], at.to(ox=o))
        if s == 1:
            total = graw[1]
            for o in range(1, nx):
                misc.got(("gx", o), gx.at[o - 1], own)
                total = total + gx[o - 1]
            graw[2] = total
            for o in (4, 3, 5, 2, 6, 1, 7):
                misc.send(("gz", o), graw.at[2], gz.at[o - 1], at.to(oz=o))
        if s == 2:
            total = graw[2]
            for o in range(1, nz):
                misc.got(("gz", o), gz.at[o - 1], own)
                total = total + gz[o - 1]
            gall[my_bit] = total
            for oy, oc in spread:
                misc.send(("gall", oy, oc), gall.at[my_bit], gall.at[my_bit], at.to(oy=oy, oc=oc))
        if s == 3:
            for oy, oc in spread:
                theirs = pl.ds((at.yr(-oy) * 2 + (c + oc) % 2) * bit, bit)
                misc.got(("gall", oy, oc), gall.at[theirs], own)
            work[:, pl.ds(0, rank)] = gall[...]
            row = lax.broadcasted_iota(jnp.int32, (rank, rank), 0)
            col = lax.broadcasted_iota(jnp.int32, (rank, rank), 1)
            work[:, pl.ds(rank, rank)] = jnp.where(row == col, 1.0, 0.0).astype(F32)

    blocks = rank // ROWS
    state = {"next": 0}

    def invert(count):
        start = state["next"]
        stop = min(blocks, start + count)
        state["next"] = stop
        if stop > start:

            def step(b, carry):
                invert_block(b, work, inv)
                return carry

            lax.fori_loop(start, stop, step, 0)

    def beside_reduce(s):
        gram_steps(s)
        invert((0, 0, 0, 1, 1, 4)[s])

    b_sum, a_sum = reduce(at, two, parts, sib, xb, zsum, zb, za, xsum, xa, make, beside_reduce)
    whole[z, x, c, pl.ds(0, FIRST)] = b_sum
    whole[z, x, c, pl.ds(FIRST, depth - FIRST)] = a_sum
    kept = {}

    def couple(value):
        high_v, low_v = split(value)
        both = dot(high_v, kept["inv"], ((1,), (1,))) + dot(low_v, kept["inv"], ((1,), (1,)))
        return both[:, :rank] + both[:, rank:]

    def beside_gather(s):
        invert((5, 0, 3, 1, 1, 0)[s])
        if s == 5:
            high_i, low_i = split(inv[...])
            kept["inv"] = jnp.concatenate([high_i, low_i], axis=0)
            left = dot(projected, inv[...], ((1,), (1,)), HIGHEST)
            left_ref[...] = left
            kept["left"] = (-0.05 * left).astype(BF16)

    def apply(cut, coupled):
        new_ref[:, cut] = blend[:, cut] + dot(kept["left"], coupled, ((1,), (1,)))

    def update(k):
        p = pair_at(k)
        cut = pl.ds(pl.multiple_of(p * wide, 128), wide)
        coupled = couple(whole[pl.ds(2 * p, 2)].reshape(wide, rank))
        squares = jnp.sum((coupled * coupled).reshape(wide // 8, 8, rank), axis=0)
        sq[0] = squares if k == 1 else sq[0] + squares
        later.append((cut, coupled.astype(BF16)))
        if k == cuts:
            for o in (2, 1, 3):
                misc.send(("sq", o), sq.at[0], sq.at[o], at.to(oy=o))
        if k != cuts - 1:
            while later:
                apply(*later.pop(0))

    later = []
    gather(at, three, whole, beside_gather, update)
    mine_coupled = couple(whole[z, x, c])
    squares = sq[0]
    for o in range(1, ny):
        misc.got(("sq", o), sq.at[o], own)
        squares = squares + sq[o]
    squares = jnp.sum(squares, axis=0, keepdims=True)
    right_ref[...] = mine_coupled * lax.rsqrt(squares + 1e-06)
    for wire in (one, two, three, misc):
        wire.drain()


def local(nz, nx, ny, momentum, gradient, right_prev):
    rows, columns = momentum.shape
    depth, rank = right_prev.shape
    rest = depth - FIRST
    bit = rank // (2 * ny)
    steps = 8 + (nx - 1) + 4 * nz + 28 + nz
    few = 2 * (ny - 1) + 1 + (nx - 1) + (nz - 1) + (2 * ny - 1) + (ny - 1)
    vmem = pltpu.VMEM
    sems = []
    for count in (steps, steps, steps, few):
        sems += [pltpu.SemaphoreType.DMA((count,)), pltpu.SemaphoreType.DMA((count,))]
    return pl.pallas_call(
        functools.partial(factors, nz, nx, ny),
        out_shape=(vmem((rows, columns), F32), vmem((rows, rank), F32), vmem((depth, rank), F32)),
        in_specs=[
            pl.BlockSpec(memory_space=pl.ANY),
            pl.BlockSpec(memory_space=pl.ANY),
            pl.BlockSpec(memory_space=pl.ANY),
        ],
        out_specs=(pl.BlockSpec(memory_space=vmem),) * 3,
        scratch_shapes=[
            vmem((rows, columns), F32),
            vmem((rows, columns), BF16),
            vmem((rows, columns), BF16),
            vmem((rows, columns), BF16),
            vmem((columns, rows), BF16),
            vmem((columns, rows), BF16),
            vmem((nz, nx, 2, depth, rank), F32),
            vmem((nz, nx, 2, depth, rank), F32),
            vmem((nz, nx, depth, rank), F32),
            vmem((nz, 3, FIRST, rank), F32),
            vmem((nz, FIRST, rank), F32),
            vmem((2, 4, FIRST, rank), F32),
            vmem((2, 4, nx, rest, rank), F32),
            vmem((nx, rest, rank), F32),
            vmem((nx - 1, rest, rank), F32),
            vmem((nz, nx, 2, depth, rank), F32),
            vmem((rows, 2 * rank), F32),
            vmem((rows, rank), F32),
            vmem((rows, rank), F32),
            vmem((ny - 1, rows // ny, rank), F32),
            vmem((rank, rank), F32),
            vmem((rank, 2 * rank), F32),
            vmem((rank, rank), F32),
            vmem((3, bit, rank), F32),
            vmem((nx - 1, bit, rank), F32),
            vmem((nz - 1, bit, rank), F32),
            vmem((rank, rank), F32),
            vmem((ny, 8, rank), F32),
            pltpu.SemaphoreType.DMA((3, nz // 2)),
            *sems,
        ],
        compiler_params=pltpu.CompilerParams(
            collective_id=0, has_side_effects=True, vmem_limit_bytes=48 * 1024 * 1024
        ),
    )(momentum, gradient, right_prev)


def solution(mesh):
    ny = mesh.shape["tensor"]
    nx = 4
    nz = mesh.shape["dp"] // (2 * nx)
    return jax.shard_map(
        functools.partial(local, nz, nx, ny),
        mesh=mesh,
        in_specs=(P("dp", "tensor"), P("dp", "tensor"), P(("tensor", "dp"), None)),
        out_specs=(P("dp", "tensor"), P("dp", None), P(("tensor", "dp"), None)),
        check_vma=False,
    )
```

```python
import functools

import jax
import jax.numpy as jnp
from jax import lax
from jax.experimental import pallas as pl
from jax.experimental.pallas import tpu as pltpu
from jax.sharding import PartitionSpec as P

HIGHEST = lax.Precision.HIGHEST
MESH = pl.DeviceIdType.MESH
F32 = jnp.float32
BF16 = jnp.bfloat16
ROWS = 8
BACK = 80
FIRST = 72
SIGNS = (1, -1)


def dot(a, b, dims, precision=None):
    return lax.dot_general(a, b, (dims, ((), ())), precision=precision, preferred_element_type=F32)


def split(value):
    high = value.astype(BF16)
    return high, (value - high.astype(F32)).astype(BF16)


class Place:
    def __init__(self, nz, nx, ny):
        self.nz, self.nx, self.ny = nz, nx, ny
        at = lax.axis_index("dp")
        self.y = lax.axis_index("tensor")
        self.z, self.x, self.c = at // (2 * nx), (at // 2) % nx, at % 2

    def zr(self, o):
        return (self.z + (o + 2 * self.nz)) % self.nz

    def xr(self, o):
        return (self.x + (o + 2 * self.nx)) % self.nx

    def yr(self, o):
        return (self.y + (o + 2 * self.ny)) % self.ny

    def to(self, oz=0, ox=0, oy=0, oc=0):
        core = (self.c + oc) % 2
        return ((self.zr(oz) * self.nx + self.xr(ox)) * 2 + core, self.yr(oy))

    def partners(self):
        out = [dict(oc=1)]
        out += [dict(ox=o) for o in range(1, self.nx)]
        out += [dict(oz=o) for o in range(1, self.nz)]
        out += [dict(oy=o, oc=k) for o in range(1, self.ny) for k in range(2)]
        return out


class Wire:
    def __init__(self, send_sems, recv_sems):
        self.sems, self.names, self.sent = (send_sems, recv_sems), {}, []

    def copy(self, name, src, dst, device):
        at = self.names.setdefault(name, len(self.names))
        return pltpu.make_async_remote_copy(
            src_ref=src,
            dst_ref=dst,
            send_sem=self.sems[0].at[at],
            recv_sem=self.sems[1].at[at],
            device_id=device,
            device_id_type=MESH,
        )

    def send(self, name, src, dst, device):
        copy = self.copy(name, src, dst, device)
        copy.start()
        self.sent.append(copy)

    def got(self, name, dst, device):
        self.copy(name, dst, dst, device).wait_recv()

    def drain(self):
        for copy in self.sent:
            copy.wait_send()
        self.sent = []


def first_rows(d, half, count=FIRST):
    if not half:
        return pl.ds(0, count)
    cut = (count // 16) * 8
    return pl.ds(0, cut) if d > 0 else pl.ds(cut, count - cut)


def some_x(d, half, nx):
    if not half:
        return pl.ds(0, nx)
    return pl.ds(0 if d > 0 else nx // 2, nx // 2)


def gather(at, wire, buf, hook, pair):
    nz, nx, z, x, c, zr, xr = at.nz, at.nx, at.z, at.x, at.c, at.zr, at.xr
    depth = buf.shape[3]
    rest = pl.ds(FIRST, depth - FIRST)
    own = at.to()

    def send(name, ref, **where):
        wire.send(name, ref, ref, at.to(**where))

    def got(name, ref):
        wire.got(name, ref, own)

    def turn(o, e, t):
        return buf.at[zr(o), xr(-e * t), c, first_rows(e, t == 2)]

    def share(o, j):
        send(("both", o, j), buf.at[zr(o), xr(-j), c, first_rows(1, False)], oc=1)

    def across(o):
        for e in SIGNS:
            send(("bx", o, e, 1), buf.at[zr(o), x, c, first_rows(e, False)], ox=e)
        share(o, 0)

    def pass_on(o):
        for e in SIGNS:
            got(("bx", o, e, 1), turn(o, e, 1))
            send(("bx", o, e, 2), buf.at[zr(o), xr(-e), c, first_rows(e, True)], ox=e)
            share(o, e % nx)

    def close(o):
        for e in SIGNS:
            got(("bx", o, e, 2), turn(o, e, 2))
        share(o, 2)
        send(("rest", o), buf.at[zr(o), :, c, rest], oc=1)

    def other(o):
        for j in range(nx):
            got(("both", o, j), buf.at[zr(o), xr(-j), 1 - c, first_rows(1, False)])
        got(("rest", o), buf.at[zr(o), :, 1 - c, rest])

    def group(d, k):
        if k < 4:
            return (0, 1, 3, 2)
        return (0, 1) if d > 0 else (3, 2)

    def straight(o):
        for j in (2, 1, 3):
            send(("bx", o, 0, j), buf.at[zr(o), x, c, first_rows(1, False)], ox=j)
        share(o, 0)

    def spread(j):
        for d in SIGNS:
            for k in (2, 1):
                send(("az", d, k, j), buf.at[z, xr(-j), c, rest], oz=d * k)

    for d in SIGNS:
        for k in (2, 1):
            send(("bz", d, k), buf.at[z, x, c, first_rows(d, False)], oz=d * k)
    for o in (2, 1, 3):
        send(("ax", o), buf.at[z, x, c, rest], ox=o)
    across(0)
    spread(0)
    hook(0)
    for d in SIGNS:
        got(("bz", d, 1), buf.at[zr(-d), x, c, first_rows(d, False)])
        across(-d % nz)
    hook(1)
    for d in SIGNS:
        got(("bz", d, 2), buf.at[zr(-2 * d), x, c, first_rows(d, False)])
        send(("bz", d, 4), buf.at[zr(-2 * d), x, c, first_rows(d, True)], oz=2 * d)
        send(("bz", d, 3), buf.at[zr(-2 * d), x, c, first_rows(d, False)], oz=d)
    pass_on(0)
    for o in (1, 3, 2):
        got(("ax", o), buf.at[z, xr(-o), c, rest])
        spread(o)
    for d in SIGNS:
        across(-2 * d % nz)
    hook(2)
    for d in SIGNS:
        pass_on(-d % nz)
    hook(3)
    for d in SIGNS:
        got(("bz", d, 3), buf.at[zr(-3 * d), x, c, first_rows(d, False)])
        across(-3 * d % nz)
    for d in SIGNS:
        got(("bz", d, 4), buf.at[zr(-4 * d), x, c, first_rows(d, True)])
    straight(4)
    for d in SIGNS:
        pass_on(-2 * d % nz)
    for j in (0, 1, 3, 2):
        for d in SIGNS:
            got(("az", d, 2, j), buf.at[zr(-2 * d), xr(-j), c, rest])
            if j in group(d, 4):
                send(("az", d, 4, j), buf.at[zr(-2 * d), xr(-j), c, rest], oz=2 * d)
            send(("az", d, 3, j), buf.at[zr(-2 * d), xr(-j), c, rest], oz=d)
    hook(4)
    close(0)
    for d in SIGNS:
        pass_on(-3 * d % nz)
    for d in SIGNS:
        for j in group(d, 1):
            got(("az", d, 1, j), buf.at[zr(-d), xr(-j), c, rest])
        close(-d % nz)
    hook(5)
    for d in SIGNS:
        close(-2 * d % nz)
    other(0)
    for d in SIGNS:
        other(-d % nz)
    pair(1)
    for d in SIGNS:
        for j in group(d, 3):
            got(("az", d, 3, j), buf.at[zr(-3 * d), xr(-j), c, rest])
        close(-3 * d % nz)
    for d in SIGNS:
        for j in group(d, 4):
            got(("az", d, 4, j), buf.at[zr(-4 * d), xr(-j), c, rest])
    send(("rest", 4), buf.at[zr(4), :, c, rest], oc=1)
    for j in (1, 3, 2):
        got(("bx", 4, 0, j), buf.at[zr(4), xr(-j), c, first_rows(1, False)])
        share(4, j)
    for d in SIGNS:
        other(-2 * d % nz)
    pair(2)
    for d in SIGNS:
        other(-3 * d % nz)
    pair(3)
    other(4)
    pair(4)


def reduce(at, wire, parts, sib, xb, zsum, zb, za, xsum, xa, make, hook):
    nz, nx, x, c, xr = at.nz, at.nx, at.x, at.c, at.xr
    depth = parts.shape[3]
    rest = pl.ds(BACK, depth - BACK)
    own = at.to()

    def term(o):
        make(o)
        wire.send(("both", o), parts.at[o, :, 1 - c], sib.at[o], at.to(oc=1))

    def combine(o):
        wire.got(("both", o), sib.at[o], own)
        parts[o, :, c] = parts[o, :, c] + sib[o]
        for e in SIGNS:
            rows = first_rows(e, True, BACK)
            wire.send(("bx", o, e, 1), parts.at[o, xr(2), c, rows], xb.at[o, 2, rows], at.to(ox=e))

    def pass_on(o):
        for i, e in enumerate(SIGNS):
            rows = first_rows(e, True, BACK)
            wire.got(("bx", o, e, 1), xb.at[o, 2, rows], own)
            parts[o, xr(e), c, rows] = parts[o, xr(e), c, rows] + xb[o, 2, rows]
            rows = first_rows(e, False, BACK)
            wire.send(("bx", o, e, 2), parts.at[o, xr(e), c, rows], xb.at[o, i], at.to(ox=e))

    def close(o):
        total = parts[o, x, c, pl.ds(0, BACK)]
        for i, e in enumerate(SIGNS):
            wire.got(("bx", o, e, 2), xb.at[o, i], own)
            total = total + xb[o, i]
        zsum[o] = total

    def send_a(i, d, k):
        xs = some_x(d, k == 4, nx)
        wire.send(("az", d, k), parts.at[d * k % nz, xs, c, rest], za.at[i, k - 1, xs], at.to(oz=d * (1, 2, 1, 2)[k - 1]))

    def got_a(i, d, k):
        xs = some_x(d, k == 4, nx)
        wire.got(("az", d, k), za.at[i, k - 1, xs], own)
        return xs

    def send_b(i, d, k):
        rows = first_rows(d, k == 4, BACK)
        wire.send(("bz", d, k), zsum.at[d * k % nz, rows], zb.at[i, k - 1, rows], at.to(oz=d * (1, 2, 1, 2)[k - 1]))

    def got_b(i, d, k):
        rows = first_rows(d, k == 4, BACK)
        wire.got(("bz", d, k), zb.at[i, k - 1, rows], own)
        return rows

    two = tuple(enumerate(SIGNS))
    term(4)
    term(3)
    combine(4)
    for i, d in two:
        send_a(i, d, 4)
    term(5)
    hook(0)
    combine(3)
    term(2)
    combine(5)
    for i, d in two:
        send_a(i, d, 3)
    term(6)
    pass_on(4)
    combine(2)
    term(1)
    combine(6)
    hook(1)
    for o in (3, 5):
        pass_on(o)
    for i, d in two:
        o = 2 * d % nz
        for k in (3, 4):
            xs = got_a(i, d, k)
            parts[o, xs, c, rest] = parts[o, xs, c, rest] + za[i, k - 1, xs]
        send_a(i, d, 2)
    term(7)
    combine(1)
    close(4)
    for i, d in two:
        send_b(i, d, 4)
    term(0)
    combine(7)
    for i, d in two:
        send_a(i, d, 1)
    for o in (2, 6):
        pass_on(o)
    combine(0)
    for o in (3, 5):
        close(o)
    for i, d in two:
        send_b(i, d, 3)
    hook(2)
    for o in (1, 7):
        pass_on(o)
    for o in (2, 6):
        close(o)
    xsum[...] = parts[0, :, c, rest]
    for i, d in two:
        for k in (1, 2):
            got_a(i, d, k)
            xsum[...] = xsum[...] + za[i, k - 1]
    for o in range(1, nx):
        wire.send(("ax", o), xsum.at[xr(o)], xa.at[o - 1], at.to(ox=o))
    for i, d in two:
        o = 2 * d % nz
        for k in (4, 3):
            rows = got_b(i, d, k)
            zsum[o, rows] = zsum[o, rows] + zb[i, k - 1, rows]
        send_b(i, d, 2)
    pass_on(0)
    hook(3)
    hook(4)
    for o in (1, 7):
        close(o)
    for i, d in two:
        send_b(i, d, 1)
    hook(5)
    close(0)
    last = xsum[x]
    for o in range(1, nx):
        wire.got(("ax", o), xa.at[o - 1], own)
        last = last + xa[o - 1]
    first = zsum[0]
    for i, d in two:
        for k in (2, 1):
            got_b(i, d, k)
            first = first + zb[i, k - 1]
    return first, last


def invert_block(b, work, out_ref):
    size = out_ref.shape[0]
    start = pl.multiple_of(b * ROWS, ROWS)
    panel = work[pl.ds(start, ROWS), :]
    first = pltpu.roll(panel[:, :size], (size - start) % size, 1)
    g = {}
    for i in range(ROWS):
        for j in range(i, ROWS):
            g[i, j] = jnp.broadcast_to(first[i : i + 1, j : j + 1], (1, size))
    scale = []
    for k in range(ROWS):
        r = lax.rsqrt(g[k, k])
        scale.append(r)
        for j in range(k + 1, ROWS):
            g[k, j] = g[k, j] * r
        for i in range(k + 1, ROWS):
            for j in range(i, ROWS):
                g[i, j] = g[i, j] - g[k, i] * g[k, j]
    done = []
    for i in range(ROWS):
        left, right = panel[i : i + 1, :size], panel[i : i + 1, size:]
        for k in range(i):
            left = left - g[k, i] * done[k][0]
            right = right - g[k, i] * done[k][1]
        done.append((left * scale[i], right * scale[i]))
    upper = jnp.concatenate([d[0] for d in done], axis=0)
    inverse = jnp.concatenate([d[1] for d in done], axis=0)
    out_ref[pl.ds(start, ROWS), :] = inverse
    both = jnp.concatenate([upper, inverse], axis=1)
    work[...] = work[...] - dot(upper, both, ((0,), (0,)), HIGHEST)


def factors(
    nz, nx, ny,
    momentum, gradient, right_prev,
    new_ref, left_ref, right_ref,
    blend, grad, high, low, high_t, low_t, right, parts, sib, xb, zsum, zb, za, xsum, xa, whole,
    acc, part, proj, yrecv, gram, work, inv, graw, gx, gz, gall, sq,
    load_sem, s1, r1, s2, r2, s3, r3, s4, r4,
):
    at = Place(nz, nx, ny)
    z, x, c, y = at.z, at.x, at.c, at.y
    own = at.to()
    rows, columns = blend.shape
    rank = proj.shape[1]
    cuts = nz // 2
    wide = columns // cuts
    block = columns // nz
    depth = right_prev.shape[0]
    share = rows // ny
    one, two, three, misc = Wire(s1, r1), Wire(s2, r2), Wire(s3, r3), Wire(s4, r4)

    first_load = pltpu.make_async_copy(right_prev, right.at[z, x, c], load_sem.at[2, 0])
    first_load.start()
    loads = []
    for i in range(cuts):
        cut = pl.ds(i * wide, wide)
        for j, (src, dst) in enumerate(((momentum, blend), (gradient, grad))):
            copy = pltpu.make_async_copy(src.at[:, cut], dst.at[:, cut], load_sem.at[j, i])
            copy.start()
            loads.append(copy)

    partners = at.partners()
    barrier = pltpu.get_barrier_semaphore()
    for where in partners:
        pl.semaphore_signal(barrier, inc=1, device_id=at.to(**where), device_id_type=MESH)

    def prepare(s, piece):
        if piece == 0:
            loads[2 * s].wait()
            loads[2 * s + 1].wait()
        tiles = wide // 128
        half = (tiles + 1) // 2

        def step(i, carry):
            cut = pl.ds(pl.multiple_of(s * wide + i * 128, 128), 128)
            value = blend[:, cut] + grad[:, cut].astype(F32)
            blend[:, cut] = value
            high[:, cut], low[:, cut] = split(value)
            high_t[cut, :], low_t[cut, :] = split(value.T)
            return carry

        lax.fori_loop(*((0, half), (half, tiles))[piece], step, 0)


    units = [(i, piece) for i in range(cuts) for piece in range(2)]
    prepare(*units.pop(0))
    first_load.wait()
    pl.semaphore_wait(barrier, len(partners))

    def pair_at(k):
        sign = 1 - 2 * ((z + 1) % 2)
        move = (0, sign, -sign, 2)[k - 1]
        return (z // 2 + move + cuts) % cuts

    def project(k):
        p = pair_at(k)
        cut = pl.ds(pl.multiple_of(p * wide, 128), wide)
        high_r, low_r = split(right[pl.ds(2 * p, 2)].reshape(wide, rank))
        both = jnp.concatenate([high_r, low_r], axis=1)
        more = dot(high[:, cut], both, ((1,), (0,))) + dot(low[:, cut], both, ((1,), (0,)))
        acc[...] = more if k == 1 else acc[...] + more

    def prepare_some(s):
        for _ in range((3, 1, 1, 1, 1, 0)[s]):
            prepare(*units.pop(0))

    gather(at, one, right, prepare_some, project)

    part[...] = acc[:, pl.ds(0, rank)] + acc[:, pl.ds(rank, rank)]
    for o in (2, 1, 3):
        to = at.yr(o)
        misc.send(("ysum", o), part.at[pl.ds(to * share, share)], yrecv.at[o - 1], at.to(oy=o))
    mine = pl.ds(y * share, share)
    own_rows = part[mine]
    for o in range(1, ny):
        misc.got(("ysum", o), yrecv.at[o - 1], own)
        own_rows = own_rows + yrecv[o - 1]
    proj[mine] = own_rows
    for o in (2, 1, 3):
        misc.send(("yall", o), proj.at[mine], proj.at[mine], at.to(oy=o))
    for o in range(1, ny):
        theirs = pl.ds(at.yr(-o) * share, share)
        misc.got(("yall", o), proj.at[theirs], own)

    projected = proj[...]
    gram[...] = dot(projected, projected, ((0,), (0,)), HIGHEST)
    bit = rank // (2 * ny)
    my_bit = pl.ds((y * 2 + c) * bit, bit)
    misc.send("gsib", gram.at[pl.ds((y * 2 + 1 - c) * bit, bit)], graw.at[0], at.to(oc=1))
    high_p, low_p = split(projected)
    pair_p = jnp.concatenate([high_p, low_p], axis=1)

    def make(o):
        cut = pl.ds(pl.multiple_of(at.zr(o) * block, 32), block)
        both = dot(high_t[cut], pair_p, ((1,), (0,))) + dot(low_t[cut], pair_p, ((1,), (0,)))
        parts[o] = (both[:, :rank] + both[:, rank:]).reshape(nx, 2, depth, rank)

    spread = [(oy, oc) for oy in range(ny) for oc in range(2) if (oy, oc) != (0, 0)]

    def gram_steps(s):
        if s == 0:
            misc.got("gsib", graw.at[0], own)
            graw[1] = graw[0] + gram[my_bit]
            for o in range(1, nx):
                misc.send(("gx", o), graw.at[1], gx.at[o - 1], at.to(ox=o))
        if s == 1:
            total = graw[1]
            for o in range(1, nx):
                misc.got(("gx", o), gx.at[o - 1], own)
                total = total + gx[o - 1]
            graw[2] = total
            for o in (4, 3, 5, 2, 6, 1, 7):
                misc.send(("gz", o), graw.at[2], gz.at[o - 1], at.to(oz=o))
        if s == 2:
            total = graw[2]
            for o in range(1, nz):
                misc.got(("gz", o), gz.at[o - 1], own)
                total = total + gz[o - 1]
            gall[my_bit] = total
            for oy, oc in spread:
                misc.send(("gall", oy, oc), gall.at[my_bit], gall.at[my_bit], at.to(oy=oy, oc=oc))
        if s == 3:
            for oy, oc in spread:
                theirs = pl.ds((at.yr(-oy) * 2 + (c + oc) % 2) * bit, bit)
                misc.got(("gall", oy, oc), gall.at[theirs], own)
            work[:, pl.ds(0, rank)] = gall[...]
            row = lax.broadcasted_iota(jnp.int32, (rank, rank), 0)
            col = lax.broadcasted_iota(jnp.int32, (rank, rank), 1)
            work[:, pl.ds(rank, rank)] = jnp.where(row == col, 1.0, 0.0).astype(F32)

    blocks = rank // ROWS
    state = {"next": 0}

    def invert(count):
        start = state["next"]
        stop = min(blocks, start + count)
        state["next"] = stop
        if stop > start:

            def step(b, carry):
                invert_block(b, work, inv)
                return carry

            lax.fori_loop(start, stop, step, 0)

    def beside_reduce(s):
        gram_steps(s)
        invert((0, 0, 0, 0, 1, 6)[s])

    b_sum, a_sum = reduce(at, two, parts, sib, xb, zsum, zb, za, xsum, xa, make, beside_reduce)
    whole[z, x, c, pl.ds(0, BACK)] = b_sum
    whole[z, x, c, pl.ds(BACK, depth - BACK)] = a_sum
    kept = {}

    def couple(value):
        high_v, low_v = split(value)
        both = dot(jnp.concatenate([high_v, low_v], axis=1), kept["inv"], ((1,), (1,)))
        return both[:, :rank] + both[:, rank:]

    def beside_gather(s):
        invert((6, 0, 3, 0, 0, 0)[s])
        if s == 5:
            high_i, low_i = split(inv[...])
            once = jnp.concatenate([high_i, low_i], axis=0)
            kept["inv"] = jnp.concatenate([once, once], axis=1)
            left = dot(projected, inv[...], ((1,), (1,)), HIGHEST)
            left_ref[...] = left
            kept["left"] = (-0.05 * left).astype(BF16)

    def apply(cut, coupled):
        new_ref[:, cut] = blend[:, cut] + dot(kept["left"], coupled, ((1,), (1,)))

    def update(k):
        p = pair_at(k)
        cut = pl.ds(pl.multiple_of(p * wide, 128), wide)
        coupled = couple(whole[pl.ds(2 * p, 2)].reshape(wide, rank))
        squares = jnp.sum((coupled * coupled).reshape(wide // 8, 8, rank), axis=0)
        sq[0] = squares if k == 1 else sq[0] + squares
        later.append((cut, coupled.astype(BF16)))
        if k == cuts:
            for o in (2, 1, 3):
                misc.send(("sq", o), sq.at[0], sq.at[o], at.to(oy=o))
        if k not in (2, 3):
            while later:
                apply(*later.pop(0))

    later = []
    gather(at, three, whole, beside_gather, update)
    mine_coupled = couple(whole[z, x, c])
    squares = sq[0]
    for o in range(1, ny):
        misc.got(("sq", o), sq.at[o], own)
        squares = squares + sq[o]
    squares = jnp.sum(squares, axis=0, keepdims=True)
    right_ref[...] = mine_coupled * lax.rsqrt(squares + 1e-06)
    for wire in (one, two, three, misc):
        wire.drain()


def local(nz, nx, ny, momentum, gradient, right_prev):
    rows, columns = momentum.shape
    depth, rank = right_prev.shape
    rest = depth - BACK
    bit = rank // (2 * ny)
    steps = 8 + (nx - 1) + 4 * nz + 28 + 5 * nz
    back = 8 + (nx - 1) + 4 * nz + 8 + nz
    few = 2 * (ny - 1) + 1 + (nx - 1) + (nz - 1) + (2 * ny - 1) + (ny - 1)
    vmem = pltpu.VMEM
    sems = []
    for count in (steps, back, steps, few):
        sems += [pltpu.SemaphoreType.DMA((count,)), pltpu.SemaphoreType.DMA((count,))]
    return pl.pallas_call(
        functools.partial(factors, nz, nx, ny),
        out_shape=(vmem((rows, columns), F32), vmem((rows, rank), F32), vmem((depth, rank), F32)),
        in_specs=[
            pl.BlockSpec(memory_space=pl.ANY),
            pl.BlockSpec(memory_space=pl.ANY),
            pl.BlockSpec(memory_space=pl.ANY),
        ],
        out_specs=(pl.BlockSpec(memory_space=vmem),) * 3,
        scratch_shapes=[
            vmem((rows, columns), F32),
            vmem((rows, columns), BF16),
            vmem((rows, columns), BF16),
            vmem((rows, columns), BF16),
            vmem((columns, rows), BF16),
            vmem((columns, rows), BF16),
            vmem((nz, nx, 2, depth, rank), F32),
            vmem((nz, nx, 2, depth, rank), F32),
            vmem((nz, nx, depth, rank), F32),
            vmem((nz, 3, BACK, rank), F32),
            vmem((nz, BACK, rank), F32),
            vmem((2, 4, BACK, rank), F32),
            vmem((2, 4, nx, rest, rank), F32),
            vmem((nx, rest, rank), F32),
            vmem((nx - 1, rest, rank), F32),
            vmem((nz, nx, 2, depth, rank), F32),
            vmem((rows, 2 * rank), F32),
            vmem((rows, rank), F32),
            vmem((rows, rank), F32),
            vmem((ny - 1, rows // ny, rank), F32),
            vmem((rank, rank), F32),
            vmem((rank, 2 * rank), F32),
            vmem((rank, rank), F32),
            vmem((3, bit, rank), F32),
            vmem((nx - 1, bit, rank), F32),
            vmem((nz - 1, bit, rank), F32),
            vmem((rank, rank), F32),
            vmem((ny, 8, rank), F32),
            pltpu.SemaphoreType.DMA((3, nz // 2)),
            *sems,
        ],
        compiler_params=pltpu.CompilerParams(
            collective_id=0, has_side_effects=True, vmem_limit_bytes=48 * 1024 * 1024
        ),
    )(momentum, gradient, right_prev)


def solution(mesh):
    ny = mesh.shape["tensor"]
    nx = 4
    nz = mesh.shape["dp"] // (2 * nx)
    return jax.shard_map(
        functools.partial(local, nz, nx, ny),
        mesh=mesh,
        in_specs=(P("dp", "tensor"), P("dp", "tensor"), P(("tensor", "dp"), None)),
        out_specs=(P("dp", "tensor"), P("dp", None), P(("tensor", "dp"), None)),
        check_vma=False,
    )
```

```python
import functools

import jax
import jax.numpy as jnp
from jax import lax
from jax.experimental import pallas as pl
from jax.experimental.pallas import tpu as pltpu
from jax.sharding import PartitionSpec as P

HIGHEST = lax.Precision.HIGHEST
MESH = pl.DeviceIdType.MESH
F32 = jnp.float32
BF16 = jnp.bfloat16
ROWS = 8
BACK = 80
FIRST = 72
SIGNS = (1, -1)


def dot(a, b, dims, precision=None):
    return lax.dot_general(a, b, (dims, ((), ())), precision=precision, preferred_element_type=F32)


def split(value):
    high = value.astype(BF16)
    return high, (value - high.astype(F32)).astype(BF16)


class Place:
    def __init__(self, nz, nx, ny):
        self.nz, self.nx, self.ny = nz, nx, ny
        at = lax.axis_index("dp")
        self.y = lax.axis_index("tensor")
        self.z, self.x, self.c = at // (2 * nx), (at // 2) % nx, at % 2

    def zr(self, o):
        return (self.z + (o + 2 * self.nz)) % self.nz

    def xr(self, o):
        return (self.x + (o + 2 * self.nx)) % self.nx

    def yr(self, o):
        return (self.y + (o + 2 * self.ny)) % self.ny

    def to(self, oz=0, ox=0, oy=0, oc=0):
        core = (self.c + oc) % 2
        return ((self.zr(oz) * self.nx + self.xr(ox)) * 2 + core, self.yr(oy))

    def partners(self):
        out = [dict(oc=1)]
        out += [dict(ox=o) for o in range(1, self.nx)]
        out += [dict(oz=o) for o in range(1, self.nz)]
        out += [dict(oy=o, oc=k) for o in range(1, self.ny) for k in range(2)]
        return out


class Wire:
    def __init__(self, send_sems, recv_sems):
        self.sems, self.names, self.sent = (send_sems, recv_sems), {}, []

    def copy(self, name, src, dst, device):
        at = self.names.setdefault(name, len(self.names))
        return pltpu.make_async_remote_copy(
            src_ref=src,
            dst_ref=dst,
            send_sem=self.sems[0].at[at],
            recv_sem=self.sems[1].at[at],
            device_id=device,
            device_id_type=MESH,
        )

    def send(self, name, src, dst, device):
        copy = self.copy(name, src, dst, device)
        copy.start()
        self.sent.append(copy)

    def got(self, name, dst, device):
        self.copy(name, dst, dst, device).wait_recv()

    def drain(self):
        for copy in self.sent:
            copy.wait_send()
        self.sent = []


def first_rows(d, half, count=FIRST):
    if not half:
        return pl.ds(0, count)
    cut = (count // 16) * 8
    return pl.ds(0, cut) if d > 0 else pl.ds(cut, count - cut)


def some_x(d, half, nx):
    if not half:
        return pl.ds(0, nx)
    return pl.ds(0 if d > 0 else nx // 2, nx // 2)


def gather(at, wire, buf, hook, pair):
    nz, nx, z, x, c, zr, xr = at.nz, at.nx, at.z, at.x, at.c, at.zr, at.xr
    depth = buf.shape[3]
    rest = pl.ds(FIRST, depth - FIRST)
    own = at.to()

    def send(name, ref, **where):
        wire.send(name, ref, ref, at.to(**where))

    def got(name, ref):
        wire.got(name, ref, own)

    def turn(o, e, t):
        return buf.at[zr(o), xr(-e * t), c, first_rows(e, t == 2)]

    def share(o, j):
        send(("both", o, j), buf.at[zr(o), xr(-j), c, first_rows(1, False)], oc=1)

    def across(o):
        for e in SIGNS:
            send(("bx", o, e, 1), buf.at[zr(o), x, c, first_rows(e, False)], ox=e)
        share(o, 0)

    def pass_on(o):
        for e in SIGNS:
            got(("bx", o, e, 1), turn(o, e, 1))
            send(("bx", o, e, 2), buf.at[zr(o), xr(-e), c, first_rows(e, True)], ox=e)
            share(o, e % nx)

    def close(o):
        for e in SIGNS:
            got(("bx", o, e, 2), turn(o, e, 2))
        share(o, 2)
        send(("rest", o), buf.at[zr(o), :, c, rest], oc=1)

    def other(o):
        for j in range(nx):
            got(("both", o, j), buf.at[zr(o), xr(-j), 1 - c, first_rows(1, False)])
        got(("rest", o), buf.at[zr(o), :, 1 - c, rest])

    def group(d, k):
        if k < 4:
            return (0, 1, 3, 2)
        return (0, 1) if d > 0 else (3, 2)

    def straight(o):
        for j in (2, 1, 3):
            send(("bx", o, 0, j), buf.at[zr(o), x, c, first_rows(1, False)], ox=j)
        share(o, 0)

    def spread(j):
        for d in SIGNS:
            for k in (2, 1):
                send(("az", d, k, j), buf.at[z, xr(-j), c, rest], oz=d * k)

    for d in SIGNS:
        for k in (2, 1):
            send(("bz", d, k), buf.at[z, x, c, first_rows(d, False)], oz=d * k)
    for o in (2, 1, 3):
        send(("ax", o), buf.at[z, x, c, rest], ox=o)
    across(0)
    spread(0)
    hook(0)
    for d in SIGNS:
        got(("bz", d, 1), buf.at[zr(-d), x, c, first_rows(d, False)])
        across(-d % nz)
    hook(1)
    for d in SIGNS:
        got(("bz", d, 2), buf.at[zr(-2 * d), x, c, first_rows(d, False)])
        send(("bz", d, 4), buf.at[zr(-2 * d), x, c, first_rows(d, True)], oz=2 * d)
        send(("bz", d, 3), buf.at[zr(-2 * d), x, c, first_rows(d, False)], oz=d)
    pass_on(0)
    for o in (1, 3, 2):
        got(("ax", o), buf.at[z, xr(-o), c, rest])
        spread(o)
    for d in SIGNS:
        across(-2 * d % nz)
    hook(2)
    for d in SIGNS:
        pass_on(-d % nz)
    hook(3)
    for d in SIGNS:
        got(("bz", d, 3), buf.at[zr(-3 * d), x, c, first_rows(d, False)])
        across(-3 * d % nz)
    for d in SIGNS:
        got(("bz", d, 4), buf.at[zr(-4 * d), x, c, first_rows(d, True)])
    straight(4)
    for d in SIGNS:
        pass_on(-2 * d % nz)
    for j in (0, 1, 3, 2):
        for d in SIGNS:
            got(("az", d, 2, j), buf.at[zr(-2 * d), xr(-j), c, rest])
            if j in group(d, 4):
                send(("az", d, 4, j), buf.at[zr(-2 * d), xr(-j), c, rest], oz=2 * d)
            send(("az", d, 3, j), buf.at[zr(-2 * d), xr(-j), c, rest], oz=d)
    hook(4)
    close(0)
    for d in SIGNS:
        pass_on(-3 * d % nz)
    for d in SIGNS:
        for j in group(d, 1):
            got(("az", d, 1, j), buf.at[zr(-d), xr(-j), c, rest])
        close(-d % nz)
    hook(5)
    for d in SIGNS:
        close(-2 * d % nz)
    other(0)
    for d in SIGNS:
        other(-d % nz)
    pair(1)
    for d in SIGNS:
        for j in group(d, 3):
            got(("az", d, 3, j), buf.at[zr(-3 * d), xr(-j), c, rest])
        close(-3 * d % nz)
    for d in SIGNS:
        for j in group(d, 4):
            got(("az", d, 4, j), buf.at[zr(-4 * d), xr(-j), c, rest])
    send(("rest", 4), buf.at[zr(4), :, c, rest], oc=1)
    for j in (1, 3, 2):
        got(("bx", 4, 0, j), buf.at[zr(4), xr(-j), c, first_rows(1, False)])
        share(4, j)
    for d in SIGNS:
        other(-2 * d % nz)
    pair(2)
    for d in SIGNS:
        other(-3 * d % nz)
    pair(3)
    other(4)
    pair(4)


def reduce(at, wire, parts, sib, xb, zsum, zb, za, xsum, xa, make, hook):
    nz, nx, x, c, xr = at.nz, at.nx, at.x, at.c, at.xr
    depth = parts.shape[3]
    rest = pl.ds(BACK, depth - BACK)
    own = at.to()

    def term(o):
        make(o)
        wire.send(("both", o), parts.at[o, :, 1 - c], sib.at[o], at.to(oc=1))

    def combine(o):
        wire.got(("both", o), sib.at[o], own)
        parts[o, :, c] = parts[o, :, c] + sib[o]
        for e in SIGNS:
            rows = first_rows(e, True, BACK)
            wire.send(("bx", o, e, 1), parts.at[o, xr(2), c, rows], xb.at[o, 2, rows], at.to(ox=e))

    def pass_on(o):
        for i, e in enumerate(SIGNS):
            rows = first_rows(e, True, BACK)
            wire.got(("bx", o, e, 1), xb.at[o, 2, rows], own)
            parts[o, xr(e), c, rows] = parts[o, xr(e), c, rows] + xb[o, 2, rows]
            rows = first_rows(e, False, BACK)
            wire.send(("bx", o, e, 2), parts.at[o, xr(e), c, rows], xb.at[o, i], at.to(ox=e))

    def close(o):
        total = parts[o, x, c, pl.ds(0, BACK)]
        for i, e in enumerate(SIGNS):
            wire.got(("bx", o, e, 2), xb.at[o, i], own)
            total = total + xb[o, i]
        zsum[o] = total

    def send_a(i, d, k):
        xs = some_x(d, k == 4, nx)
        wire.send(("az", d, k), parts.at[d * k % nz, xs, c, rest], za.at[i, k - 1, xs], at.to(oz=d * (1, 2, 1, 2)[k - 1]))

    def got_a(i, d, k):
        xs = some_x(d, k == 4, nx)
        wire.got(("az", d, k), za.at[i, k - 1, xs], own)
        return xs

    def send_b(i, d, k):
        rows = first_rows(d, k == 4, BACK)
        wire.send(("bz", d, k), zsum.at[d * k % nz, rows], zb.at[i, k - 1, rows], at.to(oz=d * (1, 2, 1, 2)[k - 1]))

    def got_b(i, d, k):
        rows = first_rows(d, k == 4, BACK)
        wire.got(("bz", d, k), zb.at[i, k - 1, rows], own)
        return rows

    two = tuple(enumerate(SIGNS))
    term(4)
    term(3)
    combine(4)
    for i, d in two:
        send_a(i, d, 4)
    term(5)
    hook(0)
    combine(3)
    term(2)
    combine(5)
    for i, d in two:
        send_a(i, d, 3)
    term(6)
    pass_on(4)
    combine(2)
    term(1)
    combine(6)
    hook(1)
    for o in (3, 5):
        pass_on(o)
    for i, d in two:
        o = 2 * d % nz
        for k in (3, 4):
            xs = got_a(i, d, k)
            parts[o, xs, c, rest] = parts[o, xs, c, rest] + za[i, k - 1, xs]
        send_a(i, d, 2)
    term(7)
    combine(1)
    close(4)
    for i, d in two:
        send_b(i, d, 4)
    term(0)
    combine(7)
    for i, d in two:
        send_a(i, d, 1)
    for o in (2, 6):
        pass_on(o)
    combine(0)
    for o in (3, 5):
        close(o)
    for i, d in two:
        send_b(i, d, 3)
    hook(2)
    for o in (1, 7):
        pass_on(o)
    for o in (2, 6):
        close(o)
    xsum[...] = parts[0, :, c, rest]
    for i, d in two:
        for k in (1, 2):
            got_a(i, d, k)
            xsum[...] = xsum[...] + za[i, k - 1]
    for o in range(1, nx):
        wire.send(("ax", o), xsum.at[xr(o)], xa.at[o - 1], at.to(ox=o))
    for i, d in two:
        o = 2 * d % nz
        for k in (4, 3):
            rows = got_b(i, d, k)
            zsum[o, rows] = zsum[o, rows] + zb[i, k - 1, rows]
        send_b(i, d, 2)
    pass_on(0)
    hook(3)
    hook(4)
    for o in (1, 7):
        close(o)
    for i, d in two:
        send_b(i, d, 1)
    hook(5)
    close(0)
    last = xsum[x]
    for o in range(1, nx):
        wire.got(("ax", o), xa.at[o - 1], own)
        last = last + xa[o - 1]
    first = zsum[0]
    for i, d in two:
        for k in (2, 1):
            got_b(i, d, k)
            first = first + zb[i, k - 1]
    return first, last


def invert_block(b, work, out_ref):
    size = out_ref.shape[0]
    start = pl.multiple_of(b * ROWS, ROWS)
    panel = work[pl.ds(start, ROWS), :]
    first = pltpu.roll(panel[:, :size], (size - start) % size, 1)
    g = {}
    for i in range(ROWS):
        for j in range(i, ROWS):
            g[i, j] = jnp.broadcast_to(first[i : i + 1, j : j + 1], (1, size))
    scale = []
    for k in range(ROWS):
        r = lax.rsqrt(g[k, k])
        scale.append(r)
        for j in range(k + 1, ROWS):
            g[k, j] = g[k, j] * r
        for i in range(k + 1, ROWS):
            for j in range(i, ROWS):
                g[i, j] = g[i, j] - g[k, i] * g[k, j]
    done = []
    for i in range(ROWS):
        left, right = panel[i : i + 1, :size], panel[i : i + 1, size:]
        for k in range(i):
            left = left - g[k, i] * done[k][0]
            right = right - g[k, i] * done[k][1]
        done.append((left * scale[i], right * scale[i]))
    upper = jnp.concatenate([d[0] for d in done], axis=0)
    inverse = jnp.concatenate([d[1] for d in done], axis=0)
    out_ref[pl.ds(start, ROWS), :] = inverse
    both = jnp.concatenate([upper, inverse], axis=1)
    work[...] = work[...] - dot(upper, both, ((0,), (0,)), HIGHEST)


def factors(
    nz, nx, ny,
    momentum, gradient, right_prev,
    new_ref, left_ref, right_ref,
    blend, grad, high, low, high_t, low_t, right, parts, sib, xb, zsum, zb, za, xsum, xa, whole,
    acc, part, proj, yrecv, gram, work, inv, graw, gx, gz, gall, sq,
    load_sem, s1, r1, s2, r2, s3, r3, s4, r4,
):
    at = Place(nz, nx, ny)
    z, x, c, y = at.z, at.x, at.c, at.y
    own = at.to()
    rows, columns = blend.shape
    rank = proj.shape[1]
    cuts = nz // 2
    wide = columns // cuts
    block = columns // nz
    depth = right_prev.shape[0]
    share = rows // ny
    one, two, three, misc = Wire(s1, r1), Wire(s2, r2), Wire(s3, r3), Wire(s4, r4)

    first_load = pltpu.make_async_copy(right_prev, right.at[z, x, c], load_sem.at[2, 0])
    first_load.start()
    loads = []
    for i in range(cuts):
        cut = pl.ds(i * wide, wide)
        for j, (src, dst) in enumerate(((momentum, blend), (gradient, grad))):
            copy = pltpu.make_async_copy(src.at[:, cut], dst.at[:, cut], load_sem.at[j, i])
            copy.start()
            loads.append(copy)

    partners = at.partners()
    barrier = pltpu.get_barrier_semaphore()
    for where in partners:
        pl.semaphore_signal(barrier, inc=1, device_id=at.to(**where), device_id_type=MESH)

    def prepare(s, piece):
        if piece == 0:
            loads[2 * s].wait()
            loads[2 * s + 1].wait()
        tiles = wide // 128
        half = (tiles + 1) // 2

        def step(i, carry):
            cut = pl.ds(pl.multiple_of(s * wide + i * 128, 128), 128)
            value = blend[:, cut] + grad[:, cut].astype(F32)
            blend[:, cut] = value
            high[:, cut], low[:, cut] = split(value)
            high_t[cut, :], low_t[cut, :] = split(value.T)
            return carry

        lax.fori_loop(*((0, half), (half, tiles))[piece], step, 0)


    units = [(i, piece) for i in range(cuts) for piece in range(2)]
    prepare(*units.pop(0))
    first_load.wait()
    pl.semaphore_wait(barrier, len(partners))

    def pair_at(k):
        sign = 1 - 2 * ((z + 1) % 2)
        move = (0, sign, -sign, 2)[k - 1]
        return (z // 2 + move + cuts) % cuts

    def project(k):
        p = pair_at(k)
        cut = pl.ds(pl.multiple_of(p * wide, 128), wide)
        high_r, low_r = split(right[pl.ds(2 * p, 2)].reshape(wide, rank))
        both = jnp.concatenate([high_r, low_r], axis=1)
        more = dot(high[:, cut], both, ((1,), (0,))) + dot(low[:, cut], both, ((1,), (0,)))
        acc[...] = more if k == 1 else acc[...] + more

    def prepare_some(s):
        for _ in range((3, 1, 1, 1, 1, 0)[s]):
            prepare(*units.pop(0))

    gather(at, one, right, prepare_some, project)

    part[...] = acc[:, pl.ds(0, rank)] + acc[:, pl.ds(rank, rank)]
    for o in (2, 1, 3):
        to = at.yr(o)
        misc.send(("ysum", o), part.at[pl.ds(to * share, share)], yrecv.at[o - 1], at.to(oy=o))
    mine = pl.ds(y * share, share)
    own_rows = part[mine]
    for o in range(1, ny):
        misc.got(("ysum", o), yrecv.at[o - 1], own)
        own_rows = own_rows + yrecv[o - 1]
    proj[mine] = own_rows
    for o in (2, 1, 3):
        misc.send(("yall", o), proj.at[mine], proj.at[mine], at.to(oy=o))
    for o in range(1, ny):
        theirs = pl.ds(at.yr(-o) * share, share)
        misc.got(("yall", o), proj.at[theirs], own)

    projected = proj[...]
    gram[...] = dot(projected, projected, ((0,), (0,)), HIGHEST)
    bit = rank // (2 * ny)
    my_bit = pl.ds((y * 2 + c) * bit, bit)
    misc.send("gsib", gram.at[pl.ds((y * 2 + 1 - c) * bit, bit)], graw.at[0], at.to(oc=1))
    high_p, low_p = split(projected)
    pair_p = jnp.concatenate([high_p, low_p], axis=1)

    def make(o):
        cut = pl.ds(pl.multiple_of(at.zr(o) * block, 32), block)
        both = dot(high_t[cut], pair_p, ((1,), (0,))) + dot(low_t[cut], pair_p, ((1,), (0,)))
        parts[o] = (both[:, :rank] + both[:, rank:]).reshape(nx, 2, depth, rank)

    spread = [(oy, oc) for oy in range(ny) for oc in range(2) if (oy, oc) != (0, 0)]

    def gram_steps(s):
        if s == 0:
            misc.got("gsib", graw.at[0], own)
            graw[1] = graw[0] + gram[my_bit]
            for o in range(1, nx):
                misc.send(("gx", o), graw.at[1], gx.at[o - 1], at.to(ox=o))
        if s == 1:
            total = graw[1]
            for o in range(1, nx):
                misc.got(("gx", o), gx.at[o - 1], own)
                total = total + gx[o - 1]
            graw[2] = total
            for o in (4, 3, 5, 2, 6, 1, 7):
                misc.send(("gz", o), graw.at[2], gz.at[o - 1], at.to(oz=o))
        if s == 2:
            total = graw[2]
            for o in range(1, nz):
                misc.got(("gz", o), gz.at[o - 1], own)
                total = total + gz[o - 1]
            gall[my_bit] = total
            for oy, oc in spread:
                misc.send(("gall", oy, oc), gall.at[my_bit], gall.at[my_bit], at.to(oy=oy, oc=oc))
        if s == 3:
            for oy, oc in spread:
                theirs = pl.ds((at.yr(-oy) * 2 + (c + oc) % 2) * bit, bit)
                misc.got(("gall", oy, oc), gall.at[theirs], own)
            work[:, pl.ds(0, rank)] = gall[...]
            row = lax.broadcasted_iota(jnp.int32, (rank, rank), 0)
            col = lax.broadcasted_iota(jnp.int32, (rank, rank), 1)
            work[:, pl.ds(rank, rank)] = jnp.where(row == col, 1.0, 0.0).astype(F32)

    blocks = rank // ROWS
    state = {"next": 0}

    def invert(count):
        start = state["next"]
        stop = min(blocks, start + count)
        state["next"] = stop
        if stop > start:

            def step(b, carry):
                invert_block(b, work, inv)
                return carry

            lax.fori_loop(start, stop, step, 0)

    def beside_reduce(s):
        gram_steps(s)
        invert((0, 0, 0, 0, 1, 5)[s])

    b_sum, a_sum = reduce(at, two, parts, sib, xb, zsum, zb, za, xsum, xa, make, beside_reduce)
    whole[z, x, c, pl.ds(0, BACK)] = b_sum
    whole[z, x, c, pl.ds(BACK, depth - BACK)] = a_sum
    kept = {}

    def couple(value):
        high_v, low_v = split(value)
        both = dot(jnp.concatenate([high_v, low_v], axis=1), kept["inv"], ((1,), (1,)))
        return both[:, :rank] + both[:, rank:]

    def beside_gather(s):
        invert((6, 0, 1, 0, 3, 0)[s])
        if s == 5:
            high_i, low_i = split(inv[...])
            once = jnp.concatenate([high_i, low_i], axis=0)
            kept["inv"] = jnp.concatenate([once, once], axis=1)
            left = dot(projected, inv[...], ((1,), (1,)), HIGHEST)
            left_ref[...] = left
            kept["left"] = (-0.05 * left).astype(BF16)

    def apply(cut, coupled):
        new_ref[:, cut] = blend[:, cut] + dot(kept["left"], coupled, ((1,), (1,)))

    def update(k):
        p = pair_at(k)
        cut = pl.ds(pl.multiple_of(p * wide, 128), wide)
        coupled = couple(whole[pl.ds(2 * p, 2)].reshape(wide, rank))
        squares = jnp.sum((coupled * coupled).reshape(wide // 8, 8, rank), axis=0)
        sq[0] = squares if k == 1 else sq[0] + squares
        later.append((cut, coupled.astype(BF16)))
        if k == cuts:
            for o in (2, 1, 3):
                misc.send(("sq", o), sq.at[0], sq.at[o], at.to(oy=o))
        if k not in (2, 3):
            while later:
                apply(*later.pop(0))

    later = []
    gather(at, three, whole, beside_gather, update)
    mine_coupled = couple(whole[z, x, c])
    squares = sq[0]
    for o in range(1, ny):
        misc.got(("sq", o), sq.at[o], own)
        squares = squares + sq[o]
    squares = jnp.sum(squares, axis=0, keepdims=True)
    right_ref[...] = mine_coupled * lax.rsqrt(squares + 1e-06)
    for wire in (one, two, three, misc):
        wire.drain()


def local(nz, nx, ny, momentum, gradient, right_prev):
    rows, columns = momentum.shape
    depth, rank = right_prev.shape
    rest = depth - BACK
    bit = rank // (2 * ny)
    steps = 8 + (nx - 1) + 4 * nz + 28 + 5 * nz
    back = 8 + (nx - 1) + 4 * nz + 8 + nz
    few = 2 * (ny - 1) + 1 + (nx - 1) + (nz - 1) + (2 * ny - 1) + (ny - 1)
    vmem = pltpu.VMEM
    sems = []
    for count in (steps, back, steps, few):
        sems += [pltpu.SemaphoreType.DMA((count,)), pltpu.SemaphoreType.DMA((count,))]
    return pl.pallas_call(
        functools.partial(factors, nz, nx, ny),
        out_shape=(vmem((rows, columns), F32), vmem((rows, rank), F32), vmem((depth, rank), F32)),
        in_specs=[
            pl.BlockSpec(memory_space=pl.ANY),
            pl.BlockSpec(memory_space=pl.ANY),
            pl.BlockSpec(memory_space=pl.ANY),
        ],
        out_specs=(pl.BlockSpec(memory_space=vmem),) * 3,
        scratch_shapes=[
            vmem((rows, columns), F32),
            vmem((rows, columns), BF16),
            vmem((rows, columns), BF16),
            vmem((rows, columns), BF16),
            vmem((columns, rows), BF16),
            vmem((columns, rows), BF16),
            vmem((nz, nx, 2, depth, rank), F32),
            vmem((nz, nx, 2, depth, rank), F32),
            vmem((nz, nx, depth, rank), F32),
            vmem((nz, 3, BACK, rank), F32),
            vmem((nz, BACK, rank), F32),
            vmem((2, 4, BACK, rank), F32),
            vmem((2, 4, nx, rest, rank), F32),
            vmem((nx, rest, rank), F32),
            vmem((nx - 1, rest, rank), F32),
            vmem((nz, nx, 2, depth, rank), F32),
            vmem((rows, 2 * rank), F32),
            vmem((rows, rank), F32),
            vmem((rows, rank), F32),
            vmem((ny - 1, rows // ny, rank), F32),
            vmem((rank, rank), F32),
            vmem((rank, 2 * rank), F32),
            vmem((rank, rank), F32),
            vmem((3, bit, rank), F32),
            vmem((nx - 1, bit, rank), F32),
            vmem((nz - 1, bit, rank), F32),
            vmem((rank, rank), F32),
            vmem((ny, 8, rank), F32),
            pltpu.SemaphoreType.DMA((3, nz // 2)),
            *sems,
        ],
        compiler_params=pltpu.CompilerParams(
            collective_id=0, has_side_effects=True, vmem_limit_bytes=48 * 1024 * 1024
        ),
    )(momentum, gradient, right_prev)


def solution(mesh):
    ny = mesh.shape["tensor"]
    nx = 4
    nz = mesh.shape["dp"] // (2 * nx)
    return jax.shard_map(
        functools.partial(local, nz, nx, ny),
        mesh=mesh,
        in_specs=(P("dp", "tensor"), P("dp", "tensor"), P(("tensor", "dp"), None)),
        out_specs=(P("dp", "tensor"), P("dp", None), P(("tensor", "dp"), None)),
        check_vma=False,
    )
```
